32 devices in a mesh: wide: 16 (over z, y, core), narrow: 2 (over x).
Axes of the slice: x: 2, y: 2, z: 4, core: 2. Of those that a mesh axis runs over, the one named last changes fastest.
Arguments:
- features: bfloat16 [32, 784, 256], P(('wide', 'narrow')), may hold values from -6 to 6
- tag_ids: int32 [32, 512], P(('wide', 'narrow')), may hold values from 0 to 31
- tag_lengths: int32 [32], P(('wide', 'narrow')), may hold values from 22 to 512, as said below
- out_cot: bfloat16 [32, 512, 512], P(('wide', 'narrow')), may hold values from -6 to 6
- proj_weight: bfloat16 [256, 512], P(None, ('wide', 'narrow')), may hold values from -0.375 to 0.375
- bn_given: bfloat16 [2, 512], P(None, ('wide', 'narrow'))
- bn_affine: bfloat16 [2, 512], P(None, ('wide', 'narrow'))
- enc_attn: bfloat16 [4, 512, 512], P(None, ('wide', 'narrow'))
- enc_vec: bfloat16 [5, 512], P(None, ('wide', 'narrow'))
- enc_ffn_in: bfloat16 [512, 1024], P(('wide', 'narrow')), may hold values from -0.25 to 0.25
- enc_hidden_bias: bfloat16 [1024], P(('wide', 'narrow')), may hold values from -4 to 4
- enc_ffn_out: bfloat16 [1024, 512], P(('wide', 'narrow')), may hold values from -0.1875 to 0.1875
- tag_table: bfloat16 [32, 512], P(None, ('wide', 'narrow')), may hold values from -6 to 6
- dec_self: bfloat16 [4, 512, 512], P(None, ('wide', 'narrow'))
- dec_cross: bfloat16 [4, 512, 512], P(None, ('wide', 'narrow'))
- dec_vec: bfloat16 [7, 512], P(None, ('wide', 'narrow'))
- dec_ffn_in: bfloat16 [512, 1024], P(('wide', 'narrow')), may hold values from -0.25 to 0.25
- dec_hidden_bias: bfloat16 [1024], P(('wide', 'narrow')), may hold values from -4 to 4
- dec_ffn_out: bfloat16 [1024, 512], P(('wide', 'narrow')), may hold values from -0.1875 to 0.1875
Outputs:
- decoded: bfloat16 [32, 512, 512], P(('wide', 'narrow'))
- grad_features: float32 [32, 784, 256], P(('wide', 'narrow'))
- grad_proj_weight: float32 [256, 512], P(None, ('wide', 'narrow'))
- grad_bn_affine: float32 [2, 512], P(None, ('wide', 'narrow'))
- grad_enc_attn: float32 [4, 512, 512], P(None, ('wide', 'narrow'))
- grad_enc_vec: float32 [5, 512], P(None, ('wide', 'narrow'))
- grad_enc_ffn_in: float32 [512, 1024], P(('wide', 'narrow'))
- grad_enc_hidden_bias: float32 [1024], P(('wide', 'narrow'))
- grad_enc_ffn_out: float32 [1024, 512], P(('wide', 'narrow'))
- grad_tag_table: float32 [32, 512], P(None, ('wide', 'narrow'))
- grad_dec_self: float32 [4, 512, 512], P(None, ('wide', 'narrow'))
- grad_dec_cross: float32 [4, 512, 512], P(None, ('wide', 'narrow'))
- grad_dec_vec: float32 [7, 512], P(None, ('wide', 'narrow'))
- grad_dec_ffn_in: float32 [512, 1024], P(('wide', 'narrow'))
- grad_dec_hidden_bias: float32 [1024], P(('wide', 'narrow'))
- grad_dec_ffn_out: float32 [1024, 512], P(('wide', 'narrow'))
The draws below stay inside these ranges and needn't reach their ends.
Inputs may be any that keep to these rules, and one draw needn't show every extreme that they name: `tag_lengths`: one table has exactly 512 tags and one exactly 22.
All inputs are finite; a program needn't handle non-finite values.
Results may differ from the reference program's by a relative error of at most 0.02.
Values may be sent and summed in bfloat16 or wider, within the bound.
A program may use at most 192 MiB of HBM per device.

```python
import math
import jax
import jax.numpy as jnp
from jax import lax

D = 512
HEADS = 8
FF = 1024
CIN = 256
VOCAB = 32
PATCH = 784
TAGS = 512
HEAD_DIM = 64
TABLES = 32


def attention_stack(key, boost):
    values = jax.random.normal(key, (4, D, D), jnp.float32) * D ** (-0.5)
    factors = jnp.array([1.0, 1.0, 1.0, boost], jnp.float32)
    return values * factors[:, None, None]


def vector_stack(key, gain_rows):
    stack_size = len(gain_rows)
    key_gain, key_shift = jax.random.split(key)
    gains = jnp.exp(jax.random.uniform(key_gain, (stack_size, D), jnp.float32, -0.5, 0.5))
    shifts = 0.3 * jax.random.normal(key_shift, (stack_size, D), jnp.float32)
    chooser = jnp.array(gain_rows, jnp.float32)[:, None]
    return chooser * gains + (1.0 - chooser) * shifts


def draw_enc_attn(key, part):
    key = jax.random.fold_in(key, 11)
    return attention_stack(key, 8.0).astype(jnp.bfloat16)


def draw_dec_self(key, part):
    key = jax.random.fold_in(key, 12)
    return attention_stack(key, 5.0).astype(jnp.bfloat16)


def draw_dec_cross(key, part):
    key = jax.random.fold_in(key, 13)
    return attention_stack(key, 8.0).astype(jnp.bfloat16)


def draw_enc_vec(key, part):
    key = jax.random.fold_in(key, 21)
    return vector_stack(key, [1.0, 0.0, 0.0, 1.0, 0.0]).astype(jnp.bfloat16)


def draw_dec_vec(key, part):
    key = jax.random.fold_in(key, 22)
    return vector_stack(key, [1.0, 0.0, 1.0, 0.0, 0.0, 1.0, 0.0]).astype(jnp.bfloat16)


def draw_bn_given(key, part):
    key = jax.random.fold_in(key, 31)
    key_mean, key_var = jax.random.split(key)
    means = 0.5 * jax.random.normal(key_mean, (1, D), jnp.float32)
    variances = jnp.exp(jax.random.uniform(key_var, (1, D), jnp.float32, -0.69, 0.69))
    return jnp.concatenate([means, variances], axis=0).astype(jnp.bfloat16)


def draw_bn_affine(key, part):
    key = jax.random.fold_in(key, 32)
    key_scale, key_shift = jax.random.split(key)
    scales = jnp.exp(jax.random.uniform(key_scale, (1, D), jnp.float32, -0.69, 0.69))
    shifts = 0.3 * jax.random.normal(key_shift, (1, D), jnp.float32)
    return jnp.concatenate([scales, shifts], axis=0).astype(jnp.bfloat16)


def draw_tag_lengths(key, part):
    key = jax.random.fold_in(key, 41)
    lowest = TAGS // 24 + 1
    key_length, key_place = jax.random.split(key)
    lengths = jax.random.randint(key_length, (TABLES,), lowest, TAGS + 1, dtype=jnp.int32)
    places = jax.random.permutation(key_place, TABLES)
    return lengths.at[places[0]].set(TAGS).at[places[1]].set(lowest).astype(jnp.int32)


def plant(result, own_key, least, top_value):
    dims = result.shape
    index_at = [jax.random.randint(jax.random.fold_in(own_key, axis), (), 0, dims[axis]) for axis in range(len(dims))]
    result = result.at[tuple(index_at)].set(least)
    longest = dims.index(max(dims))
    index_at[longest] = (index_at[longest] + 1) % dims[longest]
    return result.at[tuple(index_at)].set(top_value)


def spiked(entries, own_key, source, target, shards_of, factor):
    owner, partner = [(jnp.arange(entries.shape[position]) // (entries.shape[position] // shards_of)).reshape([-1 if axis == position else 1 for axis in range(entries.ndim)]) for position in (source, target)]
    chosen = jax.random.permutation(own_key, shards_of)[partner]
    strong = (owner == chosen) | (owner == (partner + shards_of // 2) % shards_of)
    return jnp.where(strong, factor * entries, entries)


def shard_levels(stream_key, shape, shards, smallest, top_value):
    def one(position, blocks):
        steps = jax.random.uniform(jax.random.fold_in(jax.random.fold_in(stream_key, 6), position), (blocks,), jnp.float32, smallest / len(shards), top_value / len(shards))
        return jnp.repeat(jnp.exp(steps), shape[position] // blocks).reshape((-1,) + (1,) * (len(shape) - position - 1))

    level = one(*shards[0])
    for cut in shards[1:]:
        level = level * one(*cut)
    return level


def noise(key, extent, scale, most, pieces=(), held_as=jnp.bfloat16):
    result = scale * jax.random.normal(key, extent, jnp.float32)
    if pieces:
        result = result * shard_levels(key, extent, pieces, -0.22, 0.18)
    return jnp.clip(result, -most, most).astype(held_as)


def noise_with(stream_key, dims, width, most, cuts, heavy, held_as=jnp.bfloat16):
    result = width * jax.random.normal(stream_key, dims, jnp.float32)
    if cuts:
        result = result * shard_levels(stream_key, dims, cuts, -0.22, 0.18)
    return jnp.clip(spiked(result, jax.random.fold_in(stream_key, 3), *heavy), -most, most).astype(held_as)


def setup_inputs(seed: int = 0) -> dict:
    arg_keys = jax.random.split(jax.random.key(seed), 20)
    features = noise(arg_keys[0], (TABLES, PATCH, CIN), 1.0, 6.0, ((0, 32),))
    tag_ids = plant(jax.random.randint(arg_keys[1], (TABLES, TAGS), 0, VOCAB), jax.random.fold_in(arg_keys[1], 1), 0, VOCAB - 1).astype(jnp.int32)
    tag_lengths = draw_tag_lengths(jax.random.fold_in(arg_keys[19], 71), 0)
    out_cot = noise_with(arg_keys[3], (TABLES, TAGS, D), 1.0, 6.0, ((0, 32),), (0, 2, 32, 2.75))
    proj_weight = noise(arg_keys[4], (CIN, D), CIN ** -0.5, 0.375, ((1, 32),))
    bn_given = draw_bn_given(jax.random.fold_in(arg_keys[19], 71), 0)
    bn_affine = draw_bn_affine(jax.random.fold_in(arg_keys[19], 71), 0)
    enc_attn = draw_enc_attn(jax.random.fold_in(arg_keys[19], 71), 0)
    enc_vec = draw_enc_vec(jax.random.fold_in(arg_keys[19], 71), 0)
    enc_ffn_in = noise(arg_keys[9], (D, FF), D ** -0.5, 0.25, ((0, 32),))
    enc_hidden_bias = noise(arg_keys[10], (FF,), 0.3, 4.0, ((0, 32),))
    enc_ffn_out = noise(arg_keys[11], (FF, D), FF ** -0.5, 0.1875, ((0, 32),))
    tag_table = noise(arg_keys[12], (VOCAB, D), 1.0, 6.0, ((1, 32),))
    dec_self = draw_dec_self(jax.random.fold_in(arg_keys[19], 71), 0)
    dec_cross = draw_dec_cross(jax.random.fold_in(arg_keys[19], 71), 0)
    dec_vec = draw_dec_vec(jax.random.fold_in(arg_keys[19], 71), 0)
    dec_ffn_in = noise(arg_keys[16], (D, FF), D ** -0.5, 0.25, ((0, 32),))
    dec_hidden_bias = noise(arg_keys[17], (FF,), 0.3, 4.0, ((0, 32),))
    dec_ffn_out = noise(arg_keys[18], (FF, D), FF ** -0.5, 0.1875, ((0, 32),))
    return {"features": features, "tag_ids": tag_ids, "tag_lengths": tag_lengths, "out_cot": out_cot, "proj_weight": proj_weight, "bn_given": bn_given, "bn_affine": bn_affine, "enc_attn": enc_attn, "enc_vec": enc_vec, "enc_ffn_in": enc_ffn_in, "enc_hidden_bias": enc_hidden_bias, "enc_ffn_out": enc_ffn_out, "tag_table": tag_table, "dec_self": dec_self, "dec_cross": dec_cross, "dec_vec": dec_vec, "dec_ffn_in": dec_ffn_in, "dec_hidden_bias": dec_hidden_bias, "dec_ffn_out": dec_ffn_out}


@jax.custom_vjp
def low(v):
    return lax.optimization_barrier(v.astype(jnp.bfloat16)).astype(jnp.float32)

@jax.custom_vjp
def low_back(v):
    return v

def low_keep(v):
    return (low(v), None)

def low_pass(kept, grad):
    return (grad,)

def back_keep(v):
    return (v, None)

def back_low(kept, grad):
    return (low(grad),)
low.defvjp(low_keep, low_pass)
low_back.defvjp(back_keep, back_low)

def product(left, right):
    return jnp.dot(left, right, precision=lax.Precision.HIGHEST)

def positions(row_count, model_width):
    place_index = jnp.arange(row_count, dtype=jnp.float32)[:, None]
    column = jnp.arange(model_width, dtype=jnp.int32)
    inverse = jnp.exp(-(2 * (column // 2)).astype(jnp.float32) / model_width * math.log(10000.0))
    angle_value = place_index * inverse[None, :]
    return jnp.where((column % 2 == 0)[None, :], jnp.sin(angle_value), jnp.cos(angle_value))

def layer_norm(value, gain_row, shift_row):
    centred = value - lax.optimization_barrier(jnp.mean(value, axis=-1, keepdims=True))
    spread = lax.optimization_barrier(jnp.mean(centred * centred, axis=-1, keepdims=True))
    return centred * lax.rsqrt(spread + 1e-05) * gain_row + shift_row

def attention(query_low, memory_low, weights, allowed):
    query_rows = low(low_back(product(query_low, weights[0])))
    key_rows = low(low_back(product(memory_low, weights[1])))
    value_rows = low(low_back(product(memory_low, weights[2])))
    heads_query = query_rows.reshape(query_rows.shape[0], HEADS, HEAD_DIM)
    heads_key = key_rows.reshape(key_rows.shape[0], HEADS, HEAD_DIM)
    heads_value = value_rows.reshape(value_rows.shape[0], HEADS, HEAD_DIM)
    raw_scores = low_back(jnp.einsum('qhd,khd->hqk', heads_query, heads_key, precision=lax.Precision.HIGHEST))
    scores = jnp.where(allowed[None], raw_scores * HEAD_DIM ** (-0.5), -1e+30)
    peak_score = lax.optimization_barrier(jnp.max(scores, axis=-1, keepdims=True))
    raised = jnp.exp(scores - peak_score)
    shares = raised / lax.optimization_barrier(jnp.sum(raised, axis=-1, keepdims=True))
    mixed_rows = jnp.einsum('hqk,khd->qhd', low(shares), heads_value, precision=lax.Precision.HIGHEST)
    mixed_rows = low(low_back(mixed_rows.reshape(query_rows.shape)))
    return low_back(product(mixed_rows, weights[3]))

def feed_forward(inputs_low, weight_in, hidden_bias, weight_out, out_bias):
    pre_act = low_back(product(inputs_low, weight_in)) + hidden_bias
    hidden = low(jax.nn.gelu(pre_act, approximate=False))
    return low_back(product(hidden, weight_out)) + out_bias

def table_forward(weights, features_one, ids_one, length_one):
    proj_weight, bn_given, bn_affine, enc_attn, enc_vec, enc_ffn_in, enc_hidden_bias, enc_ffn_out, tag_table, dec_self, dec_cross, dec_vec, dec_ffn_in, dec_hidden_bias, dec_ffn_out = weights
    projected = low_back(product(features_one, proj_weight))
    start = (projected - bn_given[0]) * lax.rsqrt(bn_given[1] + 1e-05) * bn_affine[0] + bn_affine[1] + positions(PATCH, D)
    start_low = low(start)
    all_pairs = jnp.ones((PATCH, PATCH), dtype=bool)
    first_out = layer_norm(start + attention(start_low, start_low, enc_attn, all_pairs), enc_vec[0], enc_vec[1])
    feed_enc = feed_forward(low(first_out), enc_ffn_in, enc_hidden_bias, enc_ffn_out, enc_vec[2])
    memory = layer_norm(first_out + feed_enc, enc_vec[3], enc_vec[4])
    memory_low = low(memory)
    chosen = (ids_one[:, None] == jnp.arange(VOCAB, dtype=jnp.int32)[None, :]).astype(jnp.float32)
    embedded = product(chosen, tag_table) + positions(TAGS, D)
    tag_order = jnp.arange(TAGS, dtype=jnp.int32)
    causal = (tag_order[None, :] <= tag_order[:, None]) & (tag_order[None, :] < length_one)
    live_rows = (tag_order < length_one).astype(jnp.float32)[:, None]
    embedded_low = low(embedded)
    second = layer_norm(embedded + attention(embedded_low, embedded_low, dec_self, causal), dec_vec[0], dec_vec[1])
    cross_pairs = jnp.ones((TAGS, PATCH), dtype=bool)
    third_out = layer_norm(second + attention(low(second), memory_low, dec_cross, cross_pairs), dec_vec[2], dec_vec[3])
    feed_dec = feed_forward(low(third_out), dec_ffn_in, dec_hidden_bias, dec_ffn_out, dec_vec[4])
    last_out = layer_norm(third_out + feed_dec, dec_vec[5], dec_vec[6])
    return last_out * live_rows

def reference(features, tag_ids, tag_lengths, out_cot, proj_weight, bn_given, bn_affine, enc_attn, enc_vec, enc_ffn_in, enc_hidden_bias, enc_ffn_out, tag_table, dec_self, dec_cross, dec_vec, dec_ffn_in, dec_hidden_bias, dec_ffn_out):
    weights = tuple((item.astype(jnp.float32) for item in (proj_weight, bn_given, bn_affine, enc_attn, enc_vec, enc_ffn_in, enc_hidden_bias, enc_ffn_out, tag_table, dec_self, dec_cross, dec_vec, dec_ffn_in, dec_hidden_bias, dec_ffn_out)))
    feature_values = features.astype(jnp.float32)

    def forward(weight_values, feature_input):

        def per_table(table_item):
            return jax.checkpoint(table_forward)(weight_values, table_item[0], table_item[1], table_item[2])
        return lax.map(per_table, (feature_input, tag_ids, tag_lengths))
    decoded_full, pullback = jax.vjp(forward, weights, feature_values)
    grad_weights, grad_feature_values = pullback(out_cot.astype(jnp.float32))
    return (decoded_full.astype(jnp.bfloat16), grad_feature_values, grad_weights[0], grad_weights[2], grad_weights[3], grad_weights[4], grad_weights[5], grad_weights[6], grad_weights[7], grad_weights[8], grad_weights[9], grad_weights[10], grad_weights[11], grad_weights[12], grad_weights[13], grad_weights[14])
```

```python
from functools import partial
import math

import jax
import jax.numpy as jnp
from jax import lax
from jax.sharding import PartitionSpec as P

HEADS = 8


def product(left, right):
    return jnp.dot(left, right, preferred_element_type=jnp.float32)


def product_inner(left, right):
    return lax.dot_general(
        left, right, (((0,), (0,)), ((), ())), preferred_element_type=jnp.float32
    )


def product_outer(left, right):
    return lax.dot_general(
        left, right, (((1,), (1,)), ((), ())), preferred_element_type=jnp.float32
    )


def positions(row_count, model_width):
    place_index = jnp.arange(row_count, dtype=jnp.float32)[:, None]
    column = jnp.arange(model_width, dtype=jnp.int32)
    inverse = jnp.exp(-(2 * (column // 2)).astype(jnp.float32) / model_width * math.log(10000.0))
    angle_value = place_index * inverse[None, :]
    return jnp.where((column % 2 == 0)[None, :], jnp.sin(angle_value), jnp.cos(angle_value))


def layer_norm(value, gain_row, shift_row):
    centred = value - jnp.mean(value, axis=-1, keepdims=True)
    spread = jnp.mean(centred * centred, axis=-1, keepdims=True)
    return centred * lax.rsqrt(spread + 1e-05) * gain_row + shift_row


def normalize_batch(projected, given_values, affine_values):
    return (projected - given_values[0]) * lax.rsqrt(given_values[1] + 1e-05) * affine_values[
        0
    ] + affine_values[1]


def split_heads(rows_value):
    return rows_value.reshape(rows_value.shape[0], HEADS, -1)


def attend_scores(query_rows, key_rows, allowed):
    heads_query = split_heads(query_rows)
    score_scale = heads_query.shape[2] ** (-0.5)
    raw_scores = jnp.einsum(
        "qhd,khd->hqk", heads_query, split_heads(key_rows), preferred_element_type=jnp.float32
    )
    return (jnp.where(allowed[None], raw_scores * score_scale, -1e30), score_scale)


def attend_forward(query_low, memory_low, weights, allowed):
    query_rows = product(query_low, weights[0]).astype(jnp.bfloat16)
    key_rows = product(memory_low, weights[1]).astype(jnp.bfloat16)
    value_rows = product(memory_low, weights[2]).astype(jnp.bfloat16)
    scores, score_scale = attend_scores(query_rows, key_rows, allowed)
    peak_score = jnp.max(scores, axis=-1, keepdims=True)
    raised = jnp.exp(scores - peak_score)
    row_total = jnp.sum(raised, axis=-1, keepdims=True)
    shares = (raised / row_total).astype(jnp.bfloat16)
    mixed_rows = jnp.einsum(
        "hqk,khd->qhd", shares, split_heads(value_rows), preferred_element_type=jnp.float32
    )
    mixed_rows = mixed_rows.reshape(query_rows.shape).astype(jnp.bfloat16)
    branch = product(mixed_rows, weights[3])
    return (branch, (query_rows, key_rows, value_rows, peak_score + jnp.log(row_total), mixed_rows))


def attend_backward(grad_branch, query_low, memory_low, weights, allowed, stored):
    query_rows, key_rows, value_rows, log_total, mixed_rows = stored
    grad_low = grad_branch.astype(jnp.bfloat16)
    grad_out_weight = product_inner(mixed_rows, grad_low)
    grad_mixed = product_outer(grad_low, weights[3]).astype(jnp.bfloat16)
    scores, score_scale = attend_scores(query_rows, key_rows, allowed)
    shares = jnp.exp(scores - log_total)
    heads_grad = split_heads(grad_mixed)
    grad_value = jnp.einsum(
        "hqk,qhd->khd", shares.astype(jnp.bfloat16), heads_grad, preferred_element_type=jnp.float32
    )
    grad_value = grad_value.reshape(value_rows.shape).astype(jnp.bfloat16)
    grad_shares = jnp.einsum(
        "qhd,khd->hqk", heads_grad, split_heads(value_rows), preferred_element_type=jnp.float32
    )
    inner_sum = jnp.sum(shares * grad_shares, axis=-1, keepdims=True)
    grad_raw = (shares * (grad_shares - inner_sum) * score_scale).astype(jnp.bfloat16)
    grad_query = jnp.einsum(
        "hqk,khd->qhd", grad_raw, split_heads(key_rows), preferred_element_type=jnp.float32
    )
    grad_query = grad_query.reshape(query_rows.shape).astype(jnp.bfloat16)
    grad_key = jnp.einsum(
        "hqk,qhd->khd", grad_raw, split_heads(query_rows), preferred_element_type=jnp.float32
    )
    grad_key = grad_key.reshape(key_rows.shape).astype(jnp.bfloat16)
    weight_grads = jnp.stack(
        [
            product_inner(query_low, grad_query),
            product_inner(memory_low, grad_key),
            product_inner(memory_low, grad_value),
            grad_out_weight,
        ]
    )
    grad_query_in = product_outer(grad_query, weights[0])
    grad_memory_in = product_outer(grad_key, weights[1]) + product_outer(grad_value, weights[2])
    return (grad_query_in, grad_memory_in, weight_grads)


def gelu_exact(value):
    return jax.nn.gelu(value, approximate=False)


def ffn_forward(inputs_low, weight_in, hidden_bias, weight_out, out_bias):
    pre_act = product(inputs_low, weight_in) + hidden_bias.astype(jnp.float32)
    hidden = gelu_exact(pre_act).astype(jnp.bfloat16)
    return (product(hidden, weight_out) + out_bias, (pre_act, hidden))


def ffn_backward(grad_out, inputs_low, weight_in, weight_out, stored):
    pre_act, hidden = stored
    grad_low = grad_out.astype(jnp.bfloat16)
    grad_weight_out = product_inner(hidden, grad_low)
    grad_out_bias = jnp.sum(grad_out, axis=0)
    grad_hidden = product_outer(grad_low, weight_out)
    grad_pre = jax.vjp(gelu_exact, pre_act)[1](grad_hidden)[0]
    grad_pre_low = grad_pre.astype(jnp.bfloat16)
    grad_hidden_bias = jnp.sum(grad_pre, axis=0)
    grad_weight_in = product_inner(inputs_low, grad_pre_low)
    grad_inputs = product_outer(grad_pre_low, weight_in)
    return (grad_inputs, (grad_weight_in, grad_hidden_bias, grad_weight_out, grad_out_bias))


def tag_masks(length_one, tag_count):
    tag_order = jnp.arange(tag_count, dtype=jnp.int32)
    causal = (tag_order[None, :] <= tag_order[:, None]) & (tag_order[None, :] < length_one)
    live_rows = (tag_order < length_one).astype(jnp.float32)[:, None]
    return (causal, live_rows)


def one_hot_rows(ids_one, vocab_size):
    return (ids_one[:, None] == jnp.arange(vocab_size, dtype=jnp.int32)[None, :]).astype(
        jnp.float32
    )


def encoder_forward(weights, features_one):
    proj_weight, bn_given, bn_affine, attn_weights, vectors, ffn_in, hidden_bias, ffn_out = weights
    vector_values = vectors.astype(jnp.float32)
    projected = product(features_one, proj_weight)
    start = normalize_batch(projected, bn_given.astype(jnp.float32), bn_affine.astype(jnp.float32))
    start = start + positions(start.shape[0], start.shape[1])
    start_low = start.astype(jnp.bfloat16)
    all_pairs = jnp.ones((start.shape[0], start.shape[0]), dtype=bool)
    branch, attn_stored = attend_forward(start_low, start_low, attn_weights, all_pairs)
    resid_one = start + branch
    first_out = layer_norm(resid_one, vector_values[0], vector_values[1])
    first_low = first_out.astype(jnp.bfloat16)
    feed_out, ffn_stored = ffn_forward(first_low, ffn_in, hidden_bias, ffn_out, vector_values[2])
    resid_two = first_out + feed_out
    memory = layer_norm(resid_two, vector_values[3], vector_values[4])
    return (
        memory,
        (projected, start_low, resid_one, first_low, resid_two, attn_stored, ffn_stored),
    )


def encoder_backward(weights, features_one, grad_memory, stored):
    proj_weight, bn_given, bn_affine, attn_weights, vectors, ffn_in, hidden_bias, ffn_out = weights
    vector_values = vectors.astype(jnp.float32)
    projected, start_low, resid_one, first_low, resid_two, attn_stored, ffn_stored = stored
    _, back_two = jax.vjp(layer_norm, resid_two, vector_values[3], vector_values[4])
    grad_resid_two, grad_gain_two, grad_shift_two = back_two(grad_memory)
    grad_first_low, ffn_grads = ffn_backward(grad_resid_two, first_low, ffn_in, ffn_out, ffn_stored)
    grad_first = grad_resid_two + grad_first_low
    _, back_one = jax.vjp(layer_norm, resid_one, vector_values[0], vector_values[1])
    grad_resid_one, grad_gain_one, grad_shift_one = back_one(grad_first)
    all_pairs = jnp.ones((start_low.shape[0], start_low.shape[0]), dtype=bool)
    grad_query_in, grad_memory_in, attn_grads = attend_backward(
        grad_resid_one, start_low, start_low, attn_weights, all_pairs, attn_stored
    )
    grad_start = grad_resid_one + grad_query_in + grad_memory_in
    given_values = bn_given.astype(jnp.float32)

    def batch_piece(value, affine_values):
        return normalize_batch(value, given_values, affine_values)

    _, back_norm = jax.vjp(batch_piece, projected, bn_affine.astype(jnp.float32))
    grad_projected, grad_affine = back_norm(grad_start)
    grad_low = grad_projected.astype(jnp.bfloat16)
    grad_proj_weight = product_inner(features_one, grad_low)
    grad_features = product_outer(grad_low, proj_weight)
    grad_weight_in, grad_hidden_bias, grad_weight_out, grad_out_bias = ffn_grads
    grad_vectors = jnp.stack(
        [grad_gain_one, grad_shift_one, grad_out_bias, grad_gain_two, grad_shift_two]
    )
    return (
        (
            grad_proj_weight,
            grad_affine,
            attn_grads,
            grad_vectors,
            grad_weight_in,
            grad_hidden_bias,
            grad_weight_out,
        ),
        grad_features,
    )


def decoder_forward(weights, memory, ids_one, length_one):
    tag_table, self_weights, cross_weights, vectors, ffn_in, hidden_bias, ffn_out = weights
    vector_values = vectors.astype(jnp.float32)
    memory_low = memory.astype(jnp.bfloat16)
    causal, live_rows = tag_masks(length_one, ids_one.shape[0])
    chosen = one_hot_rows(ids_one, tag_table.shape[0])
    embedded = jnp.dot(chosen, tag_table.astype(jnp.float32), precision=lax.Precision.HIGHEST)
    embedded = embedded + positions(embedded.shape[0], embedded.shape[1])
    embedded_low = embedded.astype(jnp.bfloat16)
    branch_self, self_stored = attend_forward(embedded_low, embedded_low, self_weights, causal)
    resid_one = embedded + branch_self
    second = layer_norm(resid_one, vector_values[0], vector_values[1])
    second_low = second.astype(jnp.bfloat16)
    cross_pairs = jnp.ones((ids_one.shape[0], memory.shape[0]), dtype=bool)
    branch_cross, cross_stored = attend_forward(second_low, memory_low, cross_weights, cross_pairs)
    resid_two = second + branch_cross
    third_out = layer_norm(resid_two, vector_values[2], vector_values[3])
    third_low = third_out.astype(jnp.bfloat16)
    feed_out, ffn_stored = ffn_forward(third_low, ffn_in, hidden_bias, ffn_out, vector_values[4])
    resid_three = third_out + feed_out
    last_out = layer_norm(resid_three, vector_values[5], vector_values[6])
    stored = (
        embedded_low,
        resid_one,
        second_low,
        resid_two,
        third_low,
        resid_three,
        self_stored,
        cross_stored,
        ffn_stored,
    )
    return (last_out * live_rows, stored)


def decoder_backward(weights, memory, ids_one, length_one, cot_one, stored):
    tag_table, self_weights, cross_weights, vectors, ffn_in, hidden_bias, ffn_out = weights
    vector_values = vectors.astype(jnp.float32)
    (
        embedded_low,
        resid_one,
        second_low,
        resid_two,
        third_low,
        resid_three,
        self_stored,
        cross_stored,
        ffn_stored,
    ) = stored
    memory_low = memory.astype(jnp.bfloat16)
    causal, live_rows = tag_masks(length_one, ids_one.shape[0])
    cross_pairs = jnp.ones((ids_one.shape[0], memory.shape[0]), dtype=bool)
    _, back_three = jax.vjp(layer_norm, resid_three, vector_values[5], vector_values[6])
    grad_resid_three, grad_gain_three, grad_shift_three = back_three(
        cot_one.astype(jnp.float32) * live_rows
    )
    grad_third_low, ffn_grads = ffn_backward(
        grad_resid_three, third_low, ffn_in, ffn_out, ffn_stored
    )
    grad_third = grad_resid_three + grad_third_low
    _, back_two = jax.vjp(layer_norm, resid_two, vector_values[2], vector_values[3])
    grad_resid_two, grad_gain_two, grad_shift_two = back_two(grad_third)
    grad_second_in, grad_memory, cross_grads = attend_backward(
        grad_resid_two, second_low, memory_low, cross_weights, cross_pairs, cross_stored
    )
    grad_second = grad_resid_two + grad_second_in
    _, back_one = jax.vjp(layer_norm, resid_one, vector_values[0], vector_values[1])
    grad_resid_one, grad_gain_one, grad_shift_one = back_one(grad_second)
    grad_query_in, grad_memory_in, self_grads = attend_backward(
        grad_resid_one, embedded_low, embedded_low, self_weights, causal, self_stored
    )
    grad_embedded = grad_resid_one + grad_query_in + grad_memory_in
    chosen = one_hot_rows(ids_one, tag_table.shape[0])
    grad_table = jnp.dot(chosen.T, grad_embedded, precision=lax.Precision.HIGHEST)
    grad_weight_in, grad_hidden_bias, grad_weight_out, grad_out_bias = ffn_grads
    grad_vectors = jnp.stack(
        [
            grad_gain_one,
            grad_shift_one,
            grad_gain_two,
            grad_shift_two,
            grad_out_bias,
            grad_gain_three,
            grad_shift_three,
        ]
    )
    return (
        (
            grad_table,
            self_grads,
            cross_grads,
            grad_vectors,
            grad_weight_in,
            grad_hidden_bias,
            grad_weight_out,
        ),
        grad_memory,
    )


AXES = ("wide", "narrow")


def pack_parameters(
    proj_weight,
    bn_given,
    bn_affine,
    enc_attn,
    enc_vec,
    enc_ffn_in,
    enc_hidden_bias,
    enc_ffn_out,
    tag_table,
    dec_self,
    dec_cross,
    dec_vec,
    dec_ffn_in,
    dec_hidden_bias,
    dec_ffn_out,
):
    rows = proj_weight.shape[1]
    width = enc_attn.shape[2]
    columns = jnp.concatenate(
        [
            proj_weight,
            bn_given,
            bn_affine,
            enc_vec,
            dec_vec,
            tag_table,
            enc_hidden_bias.reshape(rows, -1).T,
            dec_hidden_bias.reshape(rows, -1).T,
        ],
        axis=0,
    )
    columns = jnp.pad(columns, ((0, width - columns.shape[0]), (0, 0))).T
    return jnp.concatenate(
        [
            columns,
            enc_attn.reshape(4 * rows, width),
            enc_ffn_in[:, :width],
            enc_ffn_in[:, width:],
            enc_ffn_out,
            dec_self.reshape(4 * rows, width),
            dec_cross.reshape(4 * rows, width),
            dec_ffn_in[:, :width],
            dec_ffn_in[:, width:],
            dec_ffn_out,
        ],
        axis=0,
    )


def unpack_parameters(gathered, rows, channels, vocab):
    count, width = gathered.shape[0], gathered.shape[2]
    total = count * rows

    def stack(start, pieces):
        part = gathered[:, start * rows : (start + pieces) * rows]
        return part.reshape(count, pieces, rows, width).swapaxes(0, 1).reshape(pieces, total, width)

    def tall(start):
        return gathered[:, start * rows : (start + 2) * rows].reshape(2 * total, width)

    columns = stack(0, 1)[0].T
    sizes = (channels, 2, 2, 5, 7, vocab, 2, 2)
    parts, at = [], 0
    for size in sizes:
        parts.append(columns[at : at + size])
        at += size
    proj_weight, bn_given, bn_affine, enc_vec, dec_vec, tag_table, enc_hidden, dec_hidden = parts
    enc_in, dec_in = stack(5, 2), stack(17, 2)
    encoder = (
        proj_weight,
        bn_given,
        bn_affine,
        stack(1, 4),
        enc_vec,
        jnp.concatenate([enc_in[0], enc_in[1]], axis=1),
        enc_hidden.T.reshape(-1),
        tall(7),
    )
    decoder = (
        tag_table,
        stack(9, 4),
        stack(13, 4),
        dec_vec,
        jnp.concatenate([dec_in[0], dec_in[1]], axis=1),
        dec_hidden.T.reshape(-1),
        tall(19),
    )
    return encoder, decoder


def pack_gradients(encoder, decoder, count):
    proj_weight, bn_affine, enc_attn, enc_vec, enc_in, enc_hidden, enc_out = encoder
    tag_table, dec_self, dec_cross, dec_vec, dec_in, dec_hidden, dec_out = decoder
    width = enc_attn.shape[2]
    columns = jnp.concatenate(
        [
            proj_weight,
            bn_affine,
            enc_vec,
            dec_vec,
            tag_table,
            enc_hidden.reshape(width, -1).T,
            dec_hidden.reshape(width, -1).T,
        ],
        axis=0,
    )
    columns = jnp.pad(columns, ((0, width - columns.shape[0]), (0, 0))).T

    def spread(stack):
        pieces, total, _ = stack.shape
        return stack.reshape(pieces, count, total // count, width).swapaxes(0, 1).reshape(
            count, -1, width
        )

    def halves(matrix):
        return jnp.stack([matrix[:, :width], matrix[:, width:]])

    return jnp.concatenate(
        [
            spread(columns[None]),
            spread(enc_attn),
            spread(halves(enc_in)),
            enc_out.reshape(count, -1, width),
            spread(dec_self),
            spread(dec_cross),
            spread(halves(dec_in)),
            dec_out.reshape(count, -1, width),
        ],
        axis=1,
    ).astype(jnp.bfloat16)


def unpack_gradients(share, rows, channels, vocab):
    share = share.astype(jnp.float32)
    width = share.shape[1]

    def stack(start, pieces):
        return share[start * rows : (start + pieces) * rows].reshape(pieces, rows, width)

    columns = share[:rows].T
    sizes = (channels, 2, 5, 7, vocab, 2, 2)
    parts, at = [], 0
    for size in sizes:
        parts.append(columns[at : at + size])
        at += size
    proj_weight, bn_affine, enc_vec, dec_vec, tag_table, enc_hidden, dec_hidden = parts
    enc_in, dec_in = stack(5, 2), stack(17, 2)
    return (
        proj_weight,
        bn_affine,
        stack(1, 4),
        enc_vec,
        jnp.concatenate([enc_in[0], enc_in[1]], axis=1),
        enc_hidden.T.reshape(-1),
        share[7 * rows : 9 * rows],
        tag_table,
        stack(9, 4),
        stack(13, 4),
        dec_vec,
        jnp.concatenate([dec_in[0], dec_in[1]], axis=1),
        dec_hidden.T.reshape(-1),
        share[19 * rows : 21 * rows],
    )


def body(features, tag_ids, tag_lengths, out_cot, *parameters):
    rows, channels = parameters[0].shape[1], parameters[0].shape[0]
    vocab = parameters[8].shape[0]
    gathered = lax.all_gather(pack_parameters(*parameters), AXES, axis=0)
    encoder_full, decoder_full = unpack_parameters(gathered, rows, channels, vocab)
    memory, encoder_stored = encoder_forward(encoder_full, features[0])
    decoded, decoder_stored = decoder_forward(decoder_full, memory, tag_ids[0], tag_lengths[0])
    decoder_grads, grad_memory = decoder_backward(
        decoder_full, memory, tag_ids[0], tag_lengths[0], out_cot[0], decoder_stored
    )
    encoder_grads, grad_features = encoder_backward(
        encoder_full, features[0], grad_memory, encoder_stored
    )
    packed = pack_gradients(encoder_grads, decoder_grads, gathered.shape[0])
    share = lax.psum_scatter(packed, AXES, scatter_dimension=0, tiled=False)
    return (
        decoded.astype(jnp.bfloat16)[None],
        grad_features[None],
        *unpack_gradients(share, rows, channels, vocab),
    )


def solution(mesh):
    placed = (
        P(("wide", "narrow"), None, None),
        P(("wide", "narrow"), None),
        P(("wide", "narrow")),
        P(("wide", "narrow"), None, None),
        P(None, ("wide", "narrow")),
        P(None, ("wide", "narrow")),
        P(None, ("wide", "narrow")),
        P(None, ("wide", "narrow"), None),
        P(None, ("wide", "narrow")),
        P(("wide", "narrow"), None),
        P(("wide", "narrow")),
        P(("wide", "narrow"), None),
        P(None, ("wide", "narrow")),
        P(None, ("wide", "narrow"), None),
        P(None, ("wide", "narrow"), None),
        P(None, ("wide", "narrow")),
        P(("wide", "narrow"), None),
        P(("wide", "narrow")),
        P(("wide", "narrow"), None),
    )
    return jax.shard_map(
        body,
        mesh=mesh,
        in_specs=placed,
        out_specs=(
            P(("wide", "narrow"), None, None),
            P(("wide", "narrow"), None, None),
            P(None, ("wide", "narrow")),
            P(None, ("wide", "narrow")),
            P(None, ("wide", "narrow"), None),
            P(None, ("wide", "narrow")),
            P(("wide", "narrow"), None),
            P(("wide", "narrow")),
            P(("wide", "narrow"), None),
            P(None, ("wide", "narrow")),
            P(None, ("wide", "narrow"), None),
            P(None, ("wide", "narrow"), None),
            P(None, ("wide", "narrow")),
            P(("wide", "narrow"), None),
            P(("wide", "narrow")),
            P(("wide", "narrow"), None),
        ),
        check_vma=False,
    )
```

```python
from functools import partial
import math

import jax
import jax.numpy as jnp
import numpy as np
from jax import lax
from jax.experimental import pallas as pl
from jax.experimental.pallas import tpu as pltpu
from jax.sharding import PartitionSpec as P

HEADS = 8
VOCAB = 32
AXES = ("wide", "narrow")
LOW = jnp.bfloat16
WIDE = jnp.float32

MISC, ENC, ENC_IN, ENC_OUT, SELF, CROSS, DEC_IN, DEC_OUT, PIECES = 0, 1, 5, 7, 9, 13, 17, 19, 21
BN, AFFINE, ENC_VEC, DEC_VEC, TABLE, VECTOR_ROWS = 0, 2, 4, 9, 16, 128


def dot_nn(left, right):
    return lax.dot_general(left, right, (((1,), (0,)), ((), ())), preferred_element_type=WIDE)


def dot_nt(left, right):
    return lax.dot_general(left, right, (((1,), (1,)), ((), ())), preferred_element_type=WIDE)


def dot_tn(left, right):
    return lax.dot_general(left, right, (((0,), (0,)), ((), ())), preferred_element_type=WIDE)


def position_table(rows, width):
    place = np.arange(rows, dtype=np.float64)[:, None]
    column = np.arange(width)
    inverse = np.exp(-(2 * (column // 2)) / width * math.log(10000.0))
    angle = place * inverse[None, :]
    return np.where((column % 2 == 0)[None, :], np.sin(angle), np.cos(angle)).astype(np.float32)


def norm_stats(value):
    centred = value - jnp.mean(value, axis=1, keepdims=True)
    scale = lax.rsqrt(jnp.mean(centred * centred, axis=1, keepdims=True) + 1e-05)
    return centred * scale, scale


def norm_back(grad, normal, scale, gain):
    inner = grad * gain
    return scale * (
        inner
        - jnp.mean(inner, axis=1, keepdims=True)
        - normal * jnp.mean(inner * normal, axis=1, keepdims=True)
    )


def col_sum(value):
    return jnp.sum(value, axis=0, keepdims=True)


def gauss_share(value):
    return 0.5 + 0.5 * lax.erf(value * math.sqrt(0.5))


def gauss_slope(value):
    return jnp.exp(value * value * -0.5) * (1.0 / math.sqrt(2.0 * math.pi))


def two_tiles(count):
    top = (count // 2 + 15) // 16 * 16
    return [(0, top), (top, count - top)]


def pick(mask, half, value):
    zero = jnp.zeros((), value.dtype)
    return jnp.where(mask, value, zero) if half == 0 else jnp.where(mask, zero, value)


def first_half(shape):
    return lax.broadcasted_iota(jnp.int32, shape, 1) < shape[1] // 2


def attend(q_ref, k_ref, v_ref, o_ref, lse_ref, tiles, length):
    slab = 128
    half_scale = LOW(0.125)

    def pair(index, _):
        cols = pl.ds(pl.multiple_of(index * slab, slab), slab)
        for start, size, keys in tiles:
            rows = pl.ds(start, size)
            k = k_ref[0:keys, cols]
            v = v_ref[0:keys, cols]
            left_k = first_half(v.shape)
            q = q_ref[rows, cols] * half_scale
            left = first_half(q.shape)
            outs, tops, sums = [], [], []
            for half in range(2):
                s = dot_nt(pick(left, half, q), k)
                if length is not None:
                    s = mask_scores(s, start, length)
                top = jnp.max(s, axis=1, keepdims=True)
                p = jnp.exp(s - top).astype(LOW)
                ones = jnp.ones((), LOW)
                full = jnp.where(left_k, v, ones) if half == 0 else jnp.where(left_k, ones, v)
                out = dot_nn(p, full)
                outs.append(out)
                tops.append(top)
                sums.append(out[:, 64:65] if half == 0 else out[:, 0:1])
            o_ref[rows, cols] = jnp.where(left, outs[0] / sums[0], outs[1] / sums[1]).astype(LOW)
            lane = lax.broadcasted_iota(jnp.int32, (size, slab), 1) - 2 * index
            kept = jnp.where(lane == 0, tops[0] + jnp.log(sums[0]), lse_ref[rows, :])
            lse_ref[rows, :] = jnp.where(lane == 1, tops[1] + jnp.log(sums[1]), kept)
        return 0

    lax.fori_loop(0, HEADS // 2, pair, 0)


def mask_scores(s, start, length):
    query = lax.broadcasted_iota(jnp.int32, s.shape, 0) + start
    key = lax.broadcasted_iota(jnp.int32, s.shape, 1)
    return jnp.where((key <= query) & (key < length), s, -1e30)


def attend_back(
    q_ref, k_ref, v_ref, lse_ref, do_ref, dq_ref, dk_ref, dv_ref, dk_acc, dv_acc, tiles, length
):
    slab = 128
    half_scale = LOW(0.125)
    total = k_ref.shape[0]

    def pair(index, _):
        cols = pl.ds(pl.multiple_of(index * slab, slab), slab)
        first = True
        for start, size, keys in sorted(tiles, key=lambda t: -t[2]):
            rows = pl.ds(start, size)
            k = k_ref[0:keys, cols]
            v = v_ref[0:keys, cols]
            q = q_ref[rows, cols] * half_scale
            do = do_ref[rows, cols]
            lane = lax.broadcasted_iota(jnp.int32, (size, slab), 1) - 2 * index
            left = first_half(q.shape)
            grads, dks, dvs = [], [], []
            for half in range(2):
                qh, doh = pick(left, half, q), pick(left, half, do)
                s = dot_nt(qh, k)
                if length is not None:
                    s = mask_scores(s, start, length)
                lse = jnp.sum(jnp.where(lane == half, lse_ref[rows, :], 0.0), axis=1, keepdims=True)
                p = jnp.exp(s - lse)
                mixed = p * dot_nt(doh, v)
                ds = (mixed - p * jnp.sum(mixed, axis=1, keepdims=True)).astype(LOW)
                p = p.astype(LOW)
                grads.append(dot_nn(ds, k))
                dks.append(dot_tn(qh, ds))
                dvs.append(dot_tn(doh, p))
            dq_ref[rows, cols] = (jnp.where(left, grads[0], grads[1]) * 0.125).astype(LOW)
            if first:
                dk_acc[:, 0:keys] = dks[0] + dks[1]
                dv_acc[:, 0:keys] = dvs[0] + dvs[1]
            else:
                dk_acc[:, 0:keys] += dks[0] + dks[1]
                dv_acc[:, 0:keys] += dvs[0] + dvs[1]
            first = False
        dk_ref[0:total, cols] = dk_acc[:, 0:total].T.astype(LOW)
        dv_ref[0:total, cols] = dv_acc[:, 0:total].T.astype(LOW)
        return 0

    lax.fori_loop(0, HEADS // 2, pair, 0)


def layer_kernel(
    feat,
    ids,
    lens,
    cot,
    pos,
    w,
    decoded,
    gfeat,
    g,
    x,
    xl,
    q,
    k,
    v,
    o,
    lse,
    r2,
    ml,
    e,
    el,
    qs,
    ks,
    vs,
    os,
    lses,
    s2,
    sl,
    qc,
    kc,
    vc,
    oc,
    lsec,
    fl,
    hid,
    dpre,
    gl,
    do,
    dq,
    dk,
    dv,
    dm,
    dk_acc,
    dv_acc,
    vec,
    gvec,
):
    patches, width = x.shape
    tags = e.shape[0]
    channels = feat.shape[1]
    hidden = hid.shape[1]
    wide_tiles = two_tiles(patches)
    tag_tiles = two_tiles(tags)
    pltpu.sync_copy(pos, dm)
    vec[...] = w[MISC, :, channels : channels + VECTOR_ROWS].astype(WIDE).T
    gvec[...] = jnp.zeros_like(gvec)
    length = lens[0:1, 0:1]

    def row(index):
        return vec[index : index + 1, :]

    def hidden_bias(index):
        return jnp.concatenate([row(index), row(index + 1)], axis=1)

    vocab = VOCAB
    enc_hidden, dec_hidden = TABLE + vocab, TABLE + vocab + 2
    bn_scale = lax.rsqrt(row(BN + 1) + 1e-05)

    def encode_rows(start, size):
        rows = pl.ds(start, size)
        projected = dot_nt(feat[rows, :], w[MISC, :, 0:channels])
        begin = (projected - row(BN)) * bn_scale * row(AFFINE) + row(AFFINE + 1) + dm[rows, :]
        x[rows, :] = begin
        low = begin.astype(LOW)
        xl[rows, :] = low
        q[rows, :] = dot_nn(low, w[ENC]).astype(LOW)
        k[rows, :] = dot_nn(low, w[ENC + 1]).astype(LOW)
        v[rows, :] = dot_nn(low, w[ENC + 2]).astype(LOW)

    for tile in wide_tiles:
        encode_rows(*tile)
    attend(q, k, v, o, lse, [(0, patches, patches)], None)

    def encode_feed(start, size):
        rows = pl.ds(start, size)
        resid = x[rows, :] + dot_nn(o[rows, :], w[ENC + 3])
        x[rows, :] = resid
        normal, _scale = norm_stats(resid)
        first = normal * row(ENC_VEC) + row(ENC_VEC + 1)
        low = first.astype(LOW)
        total = first + row(ENC_VEC + 2)
        for half in range(2):
            pre = dot_nn(low, w[ENC_IN + half]) + row(enc_hidden + half)
            act = (pre * gauss_share(pre)).astype(LOW)
            total = total + dot_nn(act, w[ENC_OUT + half])
        r2[rows, :] = total
        normal, _scale = norm_stats(total)
        memory = normal * row(ENC_VEC + 3) + row(ENC_VEC + 4)
        ml[rows, :] = memory.astype(LOW)
        kc[rows, :] = dot_nn(ml[rows, :], w[CROSS + 1]).astype(LOW)
        vc[rows, :] = dot_nn(ml[rows, :], w[CROSS + 2]).astype(LOW)

    for tile in wide_tiles:
        encode_feed(*tile)

    onehot = (
        lax.broadcasted_iota(jnp.int32, (vocab, tags), 0) == ids[0:1, :]
    ).astype(WIDE).astype(LOW)
    table = vec[TABLE : TABLE + vocab, :].astype(LOW)
    e[...] = dot_tn(onehot, table) + dm[0:tags, :]
    el[...] = e[...].astype(LOW)
    qs[...] = dot_nn(el[...], w[SELF]).astype(LOW)
    ks[...] = dot_nn(el[...], w[SELF + 1]).astype(LOW)
    vs[...] = dot_nn(el[...], w[SELF + 2]).astype(LOW)
    causal_tiles = [(start, size, start + size) for start, size in tag_tiles]
    attend(qs, ks, vs, os, lses, causal_tiles, length)

    def decode_rows(start, size):
        rows = pl.ds(start, size)
        resid = e[rows, :] + dot_nn(os[rows, :], w[SELF + 3])
        e[rows, :] = resid
        normal, _scale = norm_stats(resid)
        second = normal * row(DEC_VEC) + row(DEC_VEC + 1)
        s2[rows, :] = second
        sl[rows, :] = second.astype(LOW)
        qc[rows, :] = dot_nn(sl[rows, :], w[CROSS]).astype(LOW)

    for tile in tag_tiles:
        decode_rows(*tile)
    attend(qc, kc, vc, oc, lsec, [(0, tags, patches)], None)

    def decode_feed(start, size):
        rows = pl.ds(start, size)
        resid = s2[rows, :] + dot_nn(oc[rows, :], w[CROSS + 3])
        normal_two, scale_two = norm_stats(resid)
        third = normal_two * row(DEC_VEC + 2) + row(DEC_VEC + 3)
        low = third.astype(LOW)
        fl[rows, :] = low
        total = third + row(DEC_VEC + 4)
        kept = []
        for half in range(2):
            pre = dot_nn(low, w[DEC_IN + half]) + row(dec_hidden + half)
            share = gauss_share(pre)
            act = (pre * share).astype(LOW)
            hid[rows, half * width : (half + 1) * width] = act
            total = total + dot_nn(act, w[DEC_OUT + half])
            kept.append(share + pre * gauss_slope(pre))
        normal, scale = norm_stats(total)
        place = lax.broadcasted_iota(jnp.int32, (size, 1), 0) + start
        live = jnp.where(place < length, 1.0, 0.0)
        decoded[rows, :] = ((normal * row(DEC_VEC + 5) + row(DEC_VEC + 6)) * live).astype(LOW)
        grad = cot[rows, :].astype(WIDE) * live
        gvec[DEC_VEC + 5 : DEC_VEC + 6, :] += col_sum(grad * normal)
        gvec[DEC_VEC + 6 : DEC_VEC + 7, :] += col_sum(grad)
        grad = norm_back(grad, normal, scale, row(DEC_VEC + 5))
        gvec[DEC_VEC + 4 : DEC_VEC + 5, :] += col_sum(grad)
        grad_low = grad.astype(LOW)
        gl[rows, :] = grad_low
        for half in range(2):
            back = dot_nt(grad_low, w[DEC_OUT + half]) * kept[half]
            gvec[dec_hidden + half : dec_hidden + half + 1, :] += col_sum(back)
            back = back.astype(LOW)
            dpre[rows, half * width : (half + 1) * width] = back
            grad = grad + dot_nt(back, w[DEC_IN + half])
        gvec[DEC_VEC + 2 : DEC_VEC + 3, :] += col_sum(grad * normal_two)
        gvec[DEC_VEC + 3 : DEC_VEC + 4, :] += col_sum(grad)
        grad = norm_back(grad, normal_two, scale_two, row(DEC_VEC + 2))
        s2[rows, :] = grad
        dq[rows, :] = grad.astype(LOW)
        do[rows, :] = dot_nt(dq[rows, :], w[CROSS + 3]).astype(LOW)

    for tile in tag_tiles:
        decode_feed(*tile)
    tag_rows = slice(0, tags)

    def weight_grad(piece, left, right):
        g[piece] = dot_tn(left, right).astype(LOW)

    for half in range(2):
        cols = slice(half * width, (half + 1) * width)
        weight_grad(DEC_IN + half, fl[tag_rows, :], dpre[tag_rows, cols])
        weight_grad(DEC_OUT + half, hid[tag_rows, cols], gl[tag_rows, :])
    weight_grad(CROSS + 3, oc[...], dq[tag_rows, :])
    attend_back(
        qc, kc, vc, lsec, do, dq, dk, dv, dk_acc, dv_acc, [(0, tags, patches)], None
    )
    weight_grad(CROSS, sl[...], dq[tag_rows, :])
    weight_grad(CROSS + 1, ml[...], dk[...])
    weight_grad(CROSS + 2, ml[...], dv[...])

    def cross_memory(start, size):
        rows = pl.ds(start, size)
        dm[rows, :] = dot_nt(dk[rows, :], w[CROSS + 1]) + dot_nt(dv[rows, :], w[CROSS + 2])

    for tile in wide_tiles:
        cross_memory(*tile)

    def self_rows(start, size):
        rows = pl.ds(start, size)
        grad = s2[rows, :] + dot_nt(dq[rows, :], w[CROSS])
        normal, scale = norm_stats(e[rows, :])
        gvec[DEC_VEC : DEC_VEC + 1, :] += col_sum(grad * normal)
        gvec[DEC_VEC + 1 : DEC_VEC + 2, :] += col_sum(grad)
        grad = norm_back(grad, normal, scale, row(DEC_VEC))
        s2[rows, :] = grad
        gl[rows, :] = grad.astype(LOW)
        do[rows, :] = dot_nt(gl[rows, :], w[SELF + 3]).astype(LOW)

    for tile in tag_tiles:
        self_rows(*tile)
    weight_grad(SELF + 3, os[...], gl[tag_rows, :])
    attend_back(qs, ks, vs, lses, do, dq, dk, dv, dk_acc, dv_acc, causal_tiles, length)
    weight_grad(SELF, el[...], dq[tag_rows, :])
    weight_grad(SELF + 1, el[...], dk[tag_rows, :])
    weight_grad(SELF + 2, el[...], dv[tag_rows, :])
    grad = (
        s2[...]
        + dot_nt(dq[tag_rows, :], w[SELF])
        + dot_nt(dk[tag_rows, :], w[SELF + 1])
        + dot_nt(dv[tag_rows, :], w[SELF + 2])
    )
    high = grad.astype(LOW)
    rest = (grad - high.astype(WIDE)).astype(LOW)
    gvec[TABLE : TABLE + vocab, :] = dot_nn(onehot, high) + dot_nn(onehot, rest)

    def encode_back(start, size):
        rows = pl.ds(start, size)
        normal, scale = norm_stats(r2[rows, :])
        grad = dm[rows, :]
        gvec[ENC_VEC + 3 : ENC_VEC + 4, :] += col_sum(grad * normal)
        gvec[ENC_VEC + 4 : ENC_VEC + 5, :] += col_sum(grad)
        grad = norm_back(grad, normal, scale, row(ENC_VEC + 3))
        gvec[ENC_VEC + 2 : ENC_VEC + 3, :] += col_sum(grad)
        grad_low = grad.astype(LOW)
        gl[rows, :] = grad_low
        normal, scale = norm_stats(x[rows, :])
        low = (normal * row(ENC_VEC) + row(ENC_VEC + 1)).astype(LOW)
        fl[rows, :] = low
        for half in range(2):
            cols = slice(half * width, (half + 1) * width)
            pre = dot_nn(low, w[ENC_IN + half]) + row(enc_hidden + half)
            share = gauss_share(pre)
            hid[rows, cols] = (pre * share).astype(LOW)
            back = dot_nt(grad_low, w[ENC_OUT + half]) * (share + pre * gauss_slope(pre))
            gvec[enc_hidden + half : enc_hidden + half + 1, :] += col_sum(back)
            back = back.astype(LOW)
            dpre[rows, cols] = back
            grad = grad + dot_nt(back, w[ENC_IN + half])
        gvec[ENC_VEC : ENC_VEC + 1, :] += col_sum(grad * normal)
        gvec[ENC_VEC + 1 : ENC_VEC + 2, :] += col_sum(grad)
        grad = norm_back(grad, normal, scale, row(ENC_VEC))
        dm[rows, :] = grad
        dq[rows, :] = grad.astype(LOW)
        do[rows, :] = dot_nt(dq[rows, :], w[ENC + 3]).astype(LOW)

    for tile in wide_tiles:
        encode_back(*tile)
    for half in range(2):
        cols = slice(half * width, (half + 1) * width)
        weight_grad(ENC_IN + half, fl[...], dpre[:, cols])
        weight_grad(ENC_OUT + half, hid[:, cols], gl[...])
    weight_grad(ENC + 3, o[...], dq[...])
    halves = [(start, size, patches) for start, size in wide_tiles]
    attend_back(q, k, v, lse, do, dq, dk, dv, dk_acc, dv_acc, halves, None)
    weight_grad(ENC, xl[...], dq[...])
    weight_grad(ENC + 1, xl[...], dk[...])
    weight_grad(ENC + 2, xl[...], dv[...])

    def project_back(start, size):
        rows = pl.ds(start, size)
        grad = (
            dm[rows, :]
            + dot_nt(dq[rows, :], w[ENC])
            + dot_nt(dk[rows, :], w[ENC + 1])
            + dot_nt(dv[rows, :], w[ENC + 2])
        )
        projected = dot_nt(feat[rows, :], w[MISC, :, 0:channels])
        gvec[AFFINE : AFFINE + 1, :] += col_sum(grad * (projected - row(BN)) * bn_scale)
        gvec[AFFINE + 1 : AFFINE + 2, :] += col_sum(grad)
        low = (grad * (bn_scale * row(AFFINE))).astype(LOW)
        gl[rows, :] = low
        gfeat[rows, :] = dot_nn(low, w[MISC, :, 0:channels])

    for tile in wide_tiles:
        project_back(*tile)
    g[MISC, :, 0:channels] = dot_tn(gl[...], feat[...]).astype(LOW)
    g[MISC, :, channels : channels + VECTOR_ROWS] = gvec[...].T.astype(LOW)
    g[MISC, :, channels + VECTOR_ROWS :] = jnp.zeros(
        (width, width - channels - VECTOR_ROWS), LOW
    )


def layer_call(features, ids, length, cot, stack, hidden):
    patches, channels = features.shape
    tags, width = cot.shape
    lens = jnp.broadcast_to(length.reshape(1, 1), (8, 128))
    pos = jnp.asarray(position_table(max(patches, tags), width))
    wide = lambda *shape: pltpu.VMEM(shape, WIDE)
    low = lambda *shape: pltpu.VMEM(shape, LOW)
    vmem = pl.BlockSpec(memory_space=pltpu.VMEM)
    return pl.pallas_call(
        layer_kernel,
        in_specs=[vmem, vmem, vmem, vmem, pl.BlockSpec(memory_space=pl.ANY), vmem],
        out_shape=(
            jax.ShapeDtypeStruct((tags, width), LOW),
            jax.ShapeDtypeStruct((patches, channels), WIDE),
            jax.ShapeDtypeStruct(stack.shape, LOW),
        ),
        scratch_shapes=[
            wide(patches, width),
            low(patches, width),
            low(patches, width),
            low(patches, width),
            low(patches, width),
            low(patches, width),
            wide(patches, 128),
            wide(patches, width),
            low(patches, width),
            wide(tags, width),
            low(tags, width),
            low(tags, width),
            low(tags, width),
            low(tags, width),
            low(tags, width),
            wide(tags, 128),
            wide(tags, width),
            low(tags, width),
            low(tags, width),
            low(patches, width),
            low(patches, width),
            low(tags, width),
            wide(tags, 128),
            low(patches, width),
            low(patches, hidden),
            low(patches, hidden),
            low(patches, width),
            low(patches, width),
            low(patches, width),
            low(patches, width),
            low(patches, width),
            wide(patches, width),
            wide(128, patches),
            wide(128, patches),
            wide(VECTOR_ROWS, width),
            wide(VECTOR_ROWS, width),
        ],
        compiler_params=pltpu.CompilerParams(vmem_limit_bytes=63 << 20),
        name="layers",
    )(features, ids, lens, cot, pos, stack)


def pack_parameters(
    proj_weight,
    bn_given,
    bn_affine,
    enc_attn,
    enc_vec,
    enc_ffn_in,
    enc_hidden_bias,
    enc_ffn_out,
    tag_table,
    dec_self,
    dec_cross,
    dec_vec,
    dec_ffn_in,
    dec_hidden_bias,
    dec_ffn_out,
):
    rows = proj_weight.shape[1]
    width = enc_attn.shape[2]
    columns = jnp.concatenate(
        [
            proj_weight,
            bn_given,
            bn_affine,
            enc_vec,
            dec_vec,
            tag_table,
            enc_hidden_bias.reshape(-1, rows),
            dec_hidden_bias.reshape(-1, rows),
        ],
        axis=0,
    )
    columns = jnp.pad(columns, ((0, width - columns.shape[0]), (0, 0))).T

    def halves(matrix):
        split = matrix.reshape(rows, -1, 2, rows)
        return split.transpose(2, 0, 1, 3).reshape(2, rows, width)

    return jnp.concatenate(
        [
            columns[None],
            enc_attn,
            halves(enc_ffn_in),
            enc_ffn_out.reshape(2, rows, width),
            dec_self,
            dec_cross,
            halves(dec_ffn_in),
            dec_ffn_out.reshape(2, rows, width),
        ],
        axis=0,
    )


def unpack_gradients(share, channels, vocab):
    share = share.astype(WIDE)
    rows, width = share.shape[1:]
    columns = share[MISC, :, 0 : channels + VECTOR_ROWS].T
    vectors = columns[channels:]

    def whole(pair):
        split = pair.reshape(2, rows, -1, rows)
        return split.transpose(1, 2, 0, 3).reshape(rows, 2 * width)

    at = TABLE + vocab
    return (
        columns[:channels],
        vectors[AFFINE : AFFINE + 2],
        share[ENC:ENC_IN],
        vectors[ENC_VEC:DEC_VEC],
        whole(share[ENC_IN:ENC_OUT]),
        vectors[at : at + 2].reshape(-1),
        share[ENC_OUT:SELF].reshape(2 * rows, width),
        vectors[TABLE:at],
        share[SELF:CROSS],
        share[CROSS:DEC_IN],
        vectors[DEC_VEC:TABLE],
        whole(share[DEC_IN:DEC_OUT]),
        vectors[at + 2 : at + 4].reshape(-1),
        share[DEC_OUT:PIECES].reshape(2 * rows, width),
    )


def body(features, tag_ids, tag_lengths, out_cot, *parameters):
    channels, vocab = parameters[0].shape[0], parameters[8].shape[0]
    hidden = parameters[5].shape[1]
    packed = pack_parameters(*parameters)
    stack = lax.all_gather(packed, AXES, axis=1, tiled=True)
    decoded, grad_features, grads = layer_call(
        features[0], tag_ids, tag_lengths, out_cot[0], stack, hidden
    )
    share = lax.psum_scatter(grads, AXES, scatter_dimension=1, tiled=True)
    return (decoded[None], grad_features[None], *unpack_gradients(share, channels, vocab))


def solution(mesh):
    placed = (
        P(("wide", "narrow"), None, None),
        P(("wide", "narrow"), None),
        P(("wide", "narrow")),
        P(("wide", "narrow"), None, None),
        P(None, ("wide", "narrow")),
        P(None, ("wide", "narrow")),
        P(None, ("wide", "narrow")),
        P(None, ("wide", "narrow"), None),
        P(None, ("wide", "narrow")),
        P(("wide", "narrow"), None),
        P(("wide", "narrow")),
        P(("wide", "narrow"), None),
        P(None, ("wide", "narrow")),
        P(None, ("wide", "narrow"), None),
        P(None, ("wide", "narrow"), None),
        P(None, ("wide", "narrow")),
        P(("wide", "narrow"), None),
        P(("wide", "narrow")),
        P(("wide", "narrow"), None),
    )
    return jax.shard_map(
        body,
        mesh=mesh,
        in_specs=placed,
        out_specs=(
            P(("wide", "narrow"), None, None),
            P(("wide", "narrow"), None, None),
            P(None, ("wide", "narrow")),
            P(None, ("wide", "narrow")),
            P(None, ("wide", "narrow"), None),
            P(None, ("wide", "narrow")),
            P(("wide", "narrow"), None),
            P(("wide", "narrow")),
            P(("wide", "narrow"), None),
            P(None, ("wide", "narrow")),
            P(None, ("wide", "narrow"), None),
            P(None, ("wide", "narrow"), None),
            P(None, ("wide", "narrow")),
            P(("wide", "narrow"), None),
            P(("wide", "narrow")),
            P(("wide", "narrow"), None),
        ),
        check_vma=False,
    )
```

```python
from functools import partial
import math

import jax
import jax.numpy as jnp
import numpy as np
from jax import lax
from jax.experimental import pallas as pl
from jax.experimental.pallas import tpu as pltpu
from jax.sharding import PartitionSpec as P

HEADS = 8
VOCAB = 32
AXES = ("wide", "narrow")
LOW = jnp.bfloat16
WIDE = jnp.float32

MISC, ENC, ENC_IN, ENC_OUT, SELF, CROSS, DEC_IN, DEC_OUT, PIECES = 0, 1, 5, 7, 9, 13, 17, 19, 21
BITS = (2,) * 5
BLOCKS = 32
BN, AFFINE, ENC_VEC, DEC_VEC, TABLE, VECTOR_ROWS = 0, 2, 4, 9, 16, 128
E1, E2, D1, D2, D3, RD3, RD2, RD1, RE2, RA, RB = range(11)
(
    AT_ENCODE,
    AT_ENC_ATTEND,
    AT_ENC_FEED,
    AT_SELF_ATTEND,
    AT_CROSS_ATTEND,
    AT_DEC_FEED,
    AT_DEC_FFN_GRADS,
    AT_CROSS_BACK,
    AT_CROSS_END,
    AT_SELF_ROWS,
    AT_CROSS_GRADS,
    AT_SELF_BACK,
    AT_SELF_END,
    AT_SELF_GRADS,
    AT_ENC_FEED_BACK,
    AT_ENC_FFN_GRADS,
    AT_ENC_BACK,
    AT_ENC_END,
    AT_ENC_GRADS,
    AT_PROJECT_BACK,
    AT_DECODE,
) = range(21)
ENC_HIDDEN, DEC_HIDDEN = TABLE + VOCAB, TABLE + VOCAB + 2


def dot_nn(left, right):
    return lax.dot_general(left, right, (((1,), (0,)), ((), ())), preferred_element_type=WIDE)


def dot_nt(left, right):
    return lax.dot_general(left, right, (((1,), (1,)), ((), ())), preferred_element_type=WIDE)


def dot_tn(left, right):
    return lax.dot_general(left, right, (((0,), (0,)), ((), ())), preferred_element_type=WIDE)


def position_table(rows, width):
    place = np.arange(rows, dtype=np.float64)[:, None]
    column = np.arange(width)
    inverse = np.exp(-(2 * (column // 2)) / width * math.log(10000.0))
    angle = place * inverse[None, :]
    return np.where((column % 2 == 0)[None, :], np.sin(angle), np.cos(angle)).astype(np.float32)


def norm_stats(value):
    centred = value - jnp.mean(value, axis=1, keepdims=True)
    scale = lax.rsqrt(jnp.mean(centred * centred, axis=1, keepdims=True) + 1e-05)
    return centred * scale, scale


def norm_back(grad, normal, scale, gain):
    inner = grad * gain
    return scale * (
        inner
        - jnp.mean(inner, axis=1, keepdims=True)
        - normal * jnp.mean(inner * normal, axis=1, keepdims=True)
    )


def col_sum(value):
    return jnp.sum(value, axis=0, keepdims=True)


def gauss_share(value):
    return 0.5 + 0.5 * lax.erf(value * math.sqrt(0.5))


def gauss_slope(value):
    return jnp.exp(value * value * -0.5) * (1.0 / math.sqrt(2.0 * math.pi))


def two_tiles(count):
    top = (count // 2 + 15) // 16 * 16
    return [(0, top), (top, count - top)]


def pick(mask, half, value):
    zero = jnp.zeros((), value.dtype)
    return jnp.where(mask, value, zero) if half == 0 else jnp.where(mask, zero, value)


def first_half(shape):
    return lax.broadcasted_iota(jnp.int32, shape, 1) < shape[1] // 2


FAR, NEAR, SIDE, CORE, ACROSS = range(5)
DEEP = (FAR, NEAR)
ROUTES = ((DEEP, (ACROSS,), (SIDE,)), (DEEP, (SIDE,), (ACROSS,)), ((ACROSS,), (SIDE,), DEEP))


def my_place():
    wide = lax.axis_index("wide")
    return (wide // 8, wide // 4 % 2, wide // 2 % 2, wide % 2, lax.axis_index("narrow"))


def flips(axes):
    if len(axes) == 1:
        return [axes]
    return [axes[:1], axes[1:], axes]


def across(place, flip):
    return tuple(1 - p if i in flip else p for i, p in enumerate(place))


def device_at(place):
    far, near, side, core, narrow = place
    return (far * 8 + near * 4 + side * 2 + core, narrow)


def greet(place):
    for flip in flips(DEEP) + [(SIDE,), (CORE,), (ACROSS,)]:
        pl.semaphore_signal(
            pltpu.get_barrier_semaphore(),
            inc=1,
            device_id=device_at(across(place, flip)),
            device_id_type=pl.DeviceIdType.MESH,
        )


def await_greetings():
    pl.semaphore_wait(pltpu.get_barrier_semaphore(), 6)


def cube(stack, pieces, place, open_axes):
    index = tuple(slice(None) if i in open_axes else p for i, p in enumerate(place))
    return stack.at[(slice(*pieces),) + index]


class Gather:
    sems = 8

    def __init__(self, stack, place, pieces, route, sends, arrivals, base):
        self.stack, self.place, self.pieces, self.route = stack, place, pieces, route
        self.sends, self.arrivals, self.base = sends, arrivals, base

    def copy(self, which, flip, place, open_axes):
        part = cube(self.stack, self.pieces, place, open_axes)
        return pltpu.make_async_remote_copy(
            src_ref=part,
            dst_ref=part,
            send_sem=self.sends.at[self.base + which],
            recv_sem=self.arrivals.at[self.base + which],
            device_id=device_at(across(self.place, flip)),
            device_id_type=pl.DeviceIdType.MESH,
        )

    def hop(self, step):
        before = self.route[:step]
        first = sum(len(flips(axes)) for axes in before)
        held = sum(before, ())
        return [
            self.copy(first + i, flip, self.place, held)
            for i, flip in enumerate(flips(self.route[step]))
        ]

    def hand(self, last):
        held = self.route[0] + self.route[1]
        if not last:
            return [self.copy(4 + len(flips(self.route[2])), (CORE,), self.place, held)]
        return [
            self.copy(5 + len(flips(self.route[2])) + i, (CORE,), across(self.place, flip), held)
            for i, flip in enumerate(flips(self.route[2]))
        ]

    def advance(self, step):
        if step:
            for copy in self.hop(step - 1):
                copy.wait_recv()
        if step < 3:
            for copy in self.hop(step):
                copy.start()
        if step >= 2:
            for copy in self.hand(step == 3):
                copy.start()

    def finish(self):
        for copy in self.hand(False) + self.hand(True):
            copy.wait_recv()

    def drain(self):
        for copy in sum([self.hop(step) for step in range(3)], []) + self.hand(False) + self.hand(True):
            copy.wait_send()


class Scatter:
    sems = 6

    def __init__(self, stack, place, slots, route, inbox, room, share, piece, sends, arrivals, base):
        self.stack, self.place, self.slots, self.piece = stack, place, slots, piece
        self.order = ((CORE,),) + tuple(reversed(route))
        self.inbox, self.room, self.share = inbox, room, share
        self.sends, self.arrivals, self.base = sends, arrivals, base

    def open_axes(self, step):
        return [a for a in range(5) if a not in sum(self.order[: step + 1], ())]

    def hop(self, step):
        first = sum(len(flips(axes)) for axes in self.order[:step])
        count = self.slots[1] - self.slots[0]
        return [
            pltpu.make_async_remote_copy(
                src_ref=cube(self.stack, self.slots, across(self.place, flip), self.open_axes(step)),
                dst_ref=self.inbox[step].at[i, self.room : self.room + count],
                send_sem=self.sends.at[self.base + first + i],
                recv_sem=self.arrivals.at[self.base + first + i],
                device_id=device_at(across(self.place, flip)),
                device_id_type=pl.DeviceIdType.MESH,
            )
            for i, flip in enumerate(flips(self.order[step]))
        ]

    def advance(self, step):
        if step:
            for copy in self.hop(step - 1):
                copy.wait_recv()
            self.add(step - 1)
        if step < 4:
            for copy in self.hop(step):
                copy.start()
        else:
            self.drain()

    def add(self, step):
        first = self.slots[0]
        for at in range(self.slots[1] - first):
            mine = cube(self.stack, (first + at, first + at + 1), self.place, self.open_axes(step))
            total = mine[...][0].astype(WIDE)
            for i in range(len(flips(self.order[step]))):
                total = total + self.inbox[step][i, self.room + at].astype(WIDE)
            if step < 3:
                mine[...] = total.astype(mine.dtype)[None]
            else:
                self.share[self.piece + at] = total

    def drain(self):
        for step in range(4):
            for copy in self.hop(step):
                copy.wait_send()


def inbox_shapes(count, route, rows, width):
    order, left, shapes = ((CORE,),) + tuple(reversed(route)), 5, []
    for axes in order:
        left -= len(axes)
        shapes.append((len(flips(axes)), count) + (2,) * left + (rows, width))
    return shapes


class Group:
    def __init__(self, runs):
        self.runs = runs

    def advance(self, step):
        for run in self.runs:
            run.advance(step)

    def finish(self):
        for run in self.runs:
            run.finish()

    def drain(self):
        for run in self.runs:
            run.drain()


def run_tick(index, ticks):
    for at, tick in enumerate(ticks):
        if tick is not None:
            pl.when(index == at)(tick)


def pair_ticks(ticks, number, count):
    return ticks[number::count]


def attend(q_ref, k_ref, v_ref, o_ref, lse_ref, tiles, length, ticks=()):
    slab = 128
    half_scale = LOW(0.125)

    def pair(index, _):
        cols = pl.ds(pl.multiple_of(index * slab, slab), slab)
        for number, (start, size, keys) in enumerate(tiles):
            run_tick(index, pair_ticks(ticks, number, len(tiles)))
            rows = pl.ds(start, size)
            k = k_ref[0:keys, cols]
            v = v_ref[0:keys, cols]
            left_k = first_half(v.shape)
            q = q_ref[rows, cols] * half_scale
            left = first_half(q.shape)
            outs, tops, sums = [], [], []
            for half in range(2):
                s = dot_nt(pick(left, half, q), k)
                if length is not None:
                    s = mask_scores(s, start, length)
                top = jnp.max(s, axis=1, keepdims=True)
                p = jnp.exp(s - top).astype(LOW)
                ones = jnp.ones((), LOW)
                full = jnp.where(left_k, v, ones) if half == 0 else jnp.where(left_k, ones, v)
                out = dot_nn(p, full)
                outs.append(out)
                tops.append(top)
                sums.append(out[:, 64:65] if half == 0 else out[:, 0:1])
            o_ref[rows, cols] = jnp.where(left, outs[0] / sums[0], outs[1] / sums[1]).astype(LOW)
            lane = lax.broadcasted_iota(jnp.int32, (size, slab), 1) - 2 * index
            kept = jnp.where(lane == 0, tops[0] + jnp.log(sums[0]), lse_ref[rows, :])
            lse_ref[rows, :] = jnp.where(lane == 1, tops[1] + jnp.log(sums[1]), kept)
        return 0

    lax.fori_loop(0, HEADS // 2, pair, 0)


def mask_scores(s, start, length):
    query = lax.broadcasted_iota(jnp.int32, s.shape, 0) + start
    key = lax.broadcasted_iota(jnp.int32, s.shape, 1)
    return jnp.where((key <= query) & (key < length), s, -1e30)


def attend_back(
    q_ref, k_ref, v_ref, lse_ref, do_ref, dq_ref, dk_ref, dv_ref, dk_acc, dv_acc, tiles, length, ticks=()
):
    slab = 128
    half_scale = LOW(0.125)
    total = k_ref.shape[0]

    def pair(index, _):
        cols = pl.ds(pl.multiple_of(index * slab, slab), slab)
        first = True
        for number, (start, size, keys) in enumerate(sorted(tiles, key=lambda t: -t[2])):
            run_tick(index, pair_ticks(ticks, number, len(tiles)))
            rows = pl.ds(start, size)
            k = k_ref[0:keys, cols]
            v = v_ref[0:keys, cols]
            q = q_ref[rows, cols] * half_scale
            do = do_ref[rows, cols]
            lane = lax.broadcasted_iota(jnp.int32, (size, slab), 1) - 2 * index
            left = first_half(q.shape)
            grads, dks, dvs = [], [], []
            for half in range(2):
                qh, doh = pick(left, half, q), pick(left, half, do)
                s = dot_nt(qh, k)
                if length is not None:
                    s = mask_scores(s, start, length)
                lse = jnp.sum(jnp.where(lane == half, lse_ref[rows, :], 0.0), axis=1, keepdims=True)
                p = jnp.exp(s - lse)
                mixed = p * dot_nt(doh, v)
                ds = (mixed - p * jnp.sum(mixed, axis=1, keepdims=True)).astype(LOW)
                p = p.astype(LOW)
                grads.append(dot_nn(ds, k))
                dks.append(dot_tn(qh, ds))
                dvs.append(dot_tn(doh, p))
            dq_ref[rows, cols] = (jnp.where(left, grads[0], grads[1]) * 0.125).astype(LOW)
            if first:
                dk_acc[:, 0:keys] = dks[0] + dks[1]
                dv_acc[:, 0:keys] = dvs[0] + dvs[1]
            else:
                dk_acc[:, 0:keys] += dks[0] + dks[1]
                dv_acc[:, 0:keys] += dvs[0] + dvs[1]
            first = False
        dk_ref[0:total, cols] = dk_acc[:, 0:total].T.astype(LOW)
        dv_ref[0:total, cols] = dv_acc[:, 0:total].T.astype(LOW)
        return 0

    lax.fori_loop(0, HEADS // 2, pair, 0)


def layer_math(feat, ids, length, cot, w, decoded, gfeat, put, net, bufs):
    (
        x, xl, q, k, v, o, lse, r2, ml, e, el, qs, ks, vs, os, lses, s2, sl, qc, kc, vc, oc, lsec,
        fl, hid, gl, do, dq, dk, dv, dm, dk_acc, dv_acc, vec, gvec, gbias, done,
    ) = bufs
    patches, width = x.shape
    tags = e.shape[0]
    channels = feat.shape[1]
    wide_tiles = two_tiles(patches)
    tag_tiles = two_tiles(tags)
    tag_rows = slice(0, tags)

    def whole(piece):
        return w[piece].reshape(width, width)

    def out_half(piece, half):
        first, second = (w[piece + i, half].reshape(16, 16, width) for i in range(2))
        return jnp.stack([first, second], axis=1).reshape(width, width)

    def put_out(piece, half, value):
        value = value.reshape((2,) * 4 + (2, 16, width))
        for i in range(2):
            put(piece + i, half, value[:, :, :, :, i])

    def row(index):
        return vec[index : index + 1, :]

    def same(shape, left, right):
        at = [lax.broadcasted_iota(jnp.int32, shape, axis) for axis in range(2)]
        return jnp.where(left(at[0]) == right(at[1]), 1.0, 0.0).astype(LOW)

    block_of = same((width, BLOCKS), lambda r: r // 16, lambda d: d)
    quarters = [same((8, BLOCKS), lambda g, i=i: 4 * g + i, lambda d: d) for i in range(4)]
    spots = [same((BLOCKS, 128), lambda u, i=i: 32 * i + u, lambda lane: lane) for i in range(4)]

    def natural_bias(columns, first):
        r = lax.broadcasted_iota(jnp.int32, (width, BLOCKS), 0)
        u = lax.broadcasted_iota(jnp.int32, (width, BLOCKS), 1)
        own = jnp.where(u < 16, columns[:, first : first + 1], columns[:, first + 1 : first + 2])
        blocks = dot_tn(block_of, jnp.where(r % 16 == u % 16, own, 0.0).astype(LOW)).astype(LOW)
        packed = sum(
            dot_nn(dot_nn(quarters[i], blocks).astype(LOW), spots[i]) for i in range(4)
        )
        return [
            jnp.concatenate([packed[4 * half + i : 4 * half + i + 1] for i in range(4)], axis=1)
            for half in range(2)
        ]

    def bias_columns(total):
        packed = jnp.concatenate([total[:, 128 * g : 128 * (g + 1)] for g in range(8)], axis=0)
        columns = 0.0
        for part in range(2):
            low = packed.astype(LOW)
            packed = packed - low.astype(WIDE)
            blocks = sum(
                dot_tn(quarters[i], dot_nt(low, spots[i]).astype(LOW)) for i in range(4)
            )
            columns = columns + dot_nn(block_of, blocks.astype(LOW))
        r = lax.broadcasted_iota(jnp.int32, (width, BLOCKS), 0)
        u = lax.broadcasted_iota(jnp.int32, (width, BLOCKS), 1)
        return [
            jnp.sum(jnp.where(u == r % 16 + 16 * i, columns, 0.0), axis=1, keepdims=True)
            for i in range(2)
        ]

    def count_up(index, value):
        gvec[index : index + 1, :] += col_sum(value)

    net.fence(E1)
    columns = whole(MISC)[:, channels : channels + VECTOR_ROWS].astype(WIDE)
    vec[...] = columns.T
    gvec[...] = jnp.zeros_like(gvec)
    gbias[...] = jnp.zeros_like(gbias)
    enc_bias = natural_bias(columns, ENC_HIDDEN)
    dec_bias = natural_bias(columns, DEC_HIDDEN)
    bn_scale = lax.rsqrt(row(BN + 1) + 1e-05)
    project = whole(MISC)[:, 0:channels]

    for number, (start, size) in enumerate(wide_tiles):
        rows = pl.ds(start, size)
        projected = dot_nt(feat[rows, :], project)
        begin = (projected - row(BN)) * bn_scale * row(AFFINE) + row(AFFINE + 1) + dm[rows, :]
        x[rows, :] = begin
        low = begin.astype(LOW)
        xl[rows, :] = low
        q[rows, :] = dot_nn(low, whole(ENC)).astype(LOW)
        k[rows, :] = dot_nn(low, whole(ENC + 1)).astype(LOW)
        v[rows, :] = dot_nn(low, whole(ENC + 2)).astype(LOW)
        net.tick(AT_ENCODE, number)
    attend(q, k, v, o, lse, [(0, patches, patches)], None, net.ticks(AT_ENC_ATTEND))
    net.fence(E2)

    for number, (start, size) in enumerate(wide_tiles):
        rows = pl.ds(start, size)
        resid = x[rows, :] + dot_nn(o[rows, :], whole(ENC + 3))
        x[rows, :] = resid
        normal, _scale = norm_stats(resid)
        first = normal * row(ENC_VEC) + row(ENC_VEC + 1)
        low = first.astype(LOW)
        total = first + row(ENC_VEC + 2)
        for half in range(2):
            pre = dot_nn(low, whole(ENC_IN + half)) + enc_bias[half]
            act = (pre * gauss_share(pre)).astype(LOW)
            total = total + dot_nn(act, out_half(ENC_OUT, half))
        r2[rows, :] = total
        normal, _scale = norm_stats(total)
        ml[rows, :] = (normal * row(ENC_VEC + 3) + row(ENC_VEC + 4)).astype(LOW)
        net.tick(AT_ENC_FEED, number)
    net.fence(D1)

    onehot = (
        lax.broadcasted_iota(jnp.int32, (VOCAB, tags), 0) == ids[0:1, :]
    ).astype(WIDE).astype(LOW)
    table = vec[TABLE : TABLE + VOCAB, :].astype(LOW)
    e[...] = dot_tn(onehot, table) + dm[0:tags, :]
    el[...] = e[...].astype(LOW)
    qs[...] = dot_nn(el[...], whole(SELF)).astype(LOW)
    ks[...] = dot_nn(el[...], whole(SELF + 1)).astype(LOW)
    vs[...] = dot_nn(el[...], whole(SELF + 2)).astype(LOW)
    causal_tiles = [(start, size, start + size) for start, size in tag_tiles]
    attend(qs, ks, vs, os, lses, causal_tiles, length, net.ticks(AT_SELF_ATTEND))
    net.fence(D2)

    for start, size in tag_tiles:
        rows = pl.ds(start, size)
        resid = e[rows, :] + dot_nn(os[rows, :], whole(SELF + 3))
        e[rows, :] = resid
        normal, _scale = norm_stats(resid)
        second = normal * row(DEC_VEC) + row(DEC_VEC + 1)
        s2[rows, :] = second
        sl[rows, :] = second.astype(LOW)
        qc[rows, :] = dot_nn(sl[rows, :], whole(CROSS)).astype(LOW)
    kc[...] = dot_nn(ml[...], whole(CROSS + 1)).astype(LOW)
    vc[...] = dot_nn(ml[...], whole(CROSS + 2)).astype(LOW)
    net.tick(AT_DECODE, 0)
    attend(qc, kc, vc, oc, lsec, [(0, tags, patches)], None, net.ticks(AT_CROSS_ATTEND))
    net.fence(D3)

    for number, (start, size) in enumerate(tag_tiles):
        rows = pl.ds(start, size)
        resid = s2[rows, :] + dot_nn(oc[rows, :], whole(CROSS + 3))
        normal_two, scale_two = norm_stats(resid)
        third = normal_two * row(DEC_VEC + 2) + row(DEC_VEC + 3)
        low = third.astype(LOW)
        fl[rows, :] = low
        total = third + row(DEC_VEC + 4)
        kept = []
        for half in range(2):
            pre = dot_nn(low, whole(DEC_IN + half)) + dec_bias[half]
            share = gauss_share(pre)
            act = (pre * share).astype(LOW)
            hid[rows, half * width : (half + 1) * width] = act
            total = total + dot_nn(act, out_half(DEC_OUT, half))
            kept.append(share + pre * gauss_slope(pre))
        normal, scale = norm_stats(total)
        place = lax.broadcasted_iota(jnp.int32, (size, 1), 0) + start
        live = jnp.where(place < length, 1.0, 0.0)
        decoded[rows, :] = ((normal * row(DEC_VEC + 5) + row(DEC_VEC + 6)) * live).astype(LOW)
        grad = cot[rows, :].astype(WIDE) * live
        count_up(DEC_VEC + 5, grad * normal)
        count_up(DEC_VEC + 6, grad)
        grad = norm_back(grad, normal, scale, row(DEC_VEC + 5))
        count_up(DEC_VEC + 4, grad)
        grad_low = grad.astype(LOW)
        gl[rows, :] = grad_low
        for half in range(2):
            back = dot_nt(grad_low, out_half(DEC_OUT, half)) * kept[half]
            gbias[1:2, half * width : (half + 1) * width] += col_sum(back)
            back = back.astype(LOW)
            (dk, dv)[half][rows, :] = back
            grad = grad + dot_nt(back, whole(DEC_IN + half))
        count_up(DEC_VEC + 2, grad * normal_two)
        count_up(DEC_VEC + 3, grad)
        grad = norm_back(grad, normal_two, scale_two, row(DEC_VEC + 2))
        s2[rows, :] = grad
        dq[rows, :] = grad.astype(LOW)
        do[rows, :] = dot_nt(dq[rows, :], whole(CROSS + 3)).astype(LOW)
        net.tick(AT_DEC_FEED, number)

    def weight_grad(piece, left, right):
        put(piece, None, dot_tn(left, right))

    for half in range(2):
        cols = slice(half * width, (half + 1) * width)
        weight_grad(DEC_IN + half, fl[tag_rows, :], (dk, dv)[half][tag_rows, :])
        put_out(DEC_OUT, half, dot_tn(hid[tag_rows, cols], gl[tag_rows, :]))
    net.tick(AT_DEC_FFN_GRADS, 0)
    weight_grad(CROSS + 3, oc[...], dq[tag_rows, :])
    attend_back(
        qc, kc, vc, lsec, do, dq, dk, dv, dk_acc, dv_acc, [(0, tags, patches)], None,
        net.ticks(AT_CROSS_BACK),
    )
    net.tick(AT_CROSS_END, 0)
    for start, size in wide_tiles:
        rows = pl.ds(start, size)
        dm[rows, :] = dot_nt(dk[rows, :], whole(CROSS + 1)) + dot_nt(dv[rows, :], whole(CROSS + 2))
    for start, size in tag_tiles:
        rows = pl.ds(start, size)
        grad = s2[rows, :] + dot_nt(dq[rows, :], whole(CROSS))
        normal, scale = norm_stats(e[rows, :])
        count_up(DEC_VEC, grad * normal)
        count_up(DEC_VEC + 1, grad)
        grad = norm_back(grad, normal, scale, row(DEC_VEC))
        s2[rows, :] = grad
        gl[rows, :] = grad.astype(LOW)
        do[rows, :] = dot_nt(gl[rows, :], whole(SELF + 3)).astype(LOW)
    net.tick(AT_SELF_ROWS, 0)
    weight_grad(CROSS, sl[...], dq[tag_rows, :])
    weight_grad(CROSS + 1, ml[...], dk[...])
    weight_grad(CROSS + 2, ml[...], dv[...])
    net.tick(AT_CROSS_GRADS, 0)
    weight_grad(SELF + 3, os[...], gl[tag_rows, :])
    attend_back(
        qs, ks, vs, lses, do, dq, dk, dv, dk_acc, dv_acc, causal_tiles, length,
        net.ticks(AT_SELF_BACK),
    )
    net.tick(AT_SELF_END, 0)
    grad = (
        s2[...]
        + dot_nt(dq[tag_rows, :], whole(SELF))
        + dot_nt(dk[tag_rows, :], whole(SELF + 1))
        + dot_nt(dv[tag_rows, :], whole(SELF + 2))
    )
    high = grad.astype(LOW)
    rest = (grad - high.astype(WIDE)).astype(LOW)
    gvec[TABLE : TABLE + VOCAB, :] = dot_nn(onehot, high) + dot_nn(onehot, rest)
    weight_grad(SELF, el[...], dq[tag_rows, :])
    weight_grad(SELF + 1, el[...], dk[tag_rows, :])
    weight_grad(SELF + 2, el[...], dv[tag_rows, :])
    net.tick(AT_SELF_GRADS, 0)

    for number, (start, size) in enumerate(wide_tiles):
        rows = pl.ds(start, size)
        normal, scale = norm_stats(r2[rows, :])
        grad = dm[rows, :]
        count_up(ENC_VEC + 3, grad * normal)
        count_up(ENC_VEC + 4, grad)
        grad = norm_back(grad, normal, scale, row(ENC_VEC + 3))
        count_up(ENC_VEC + 2, grad)
        grad_low = grad.astype(LOW)
        gl[rows, :] = grad_low
        normal, scale = norm_stats(x[rows, :])
        low = (normal * row(ENC_VEC) + row(ENC_VEC + 1)).astype(LOW)
        fl[rows, :] = low
        for half in range(2):
            cols = slice(half * width, (half + 1) * width)
            pre = dot_nn(low, whole(ENC_IN + half)) + enc_bias[half]
            share = gauss_share(pre)
            (kc, vc)[half][rows, :] = (pre * share).astype(LOW)
            back = dot_nt(grad_low, out_half(ENC_OUT, half)) * (share + pre * gauss_slope(pre))
            gbias[0:1, cols] += col_sum(back)
            back = back.astype(LOW)
            (dk, dv)[half][rows, :] = back
            grad = grad + dot_nt(back, whole(ENC_IN + half))
        count_up(ENC_VEC, grad * normal)
        count_up(ENC_VEC + 1, grad)
        grad = norm_back(grad, normal, scale, row(ENC_VEC))
        dm[rows, :] = grad
        dq[rows, :] = grad.astype(LOW)
        do[rows, :] = dot_nt(dq[rows, :], whole(ENC + 3)).astype(LOW)
        net.tick(AT_ENC_FEED_BACK, number)
    for half in range(2):
        weight_grad(ENC_IN + half, fl[...], (dk, dv)[half][...])
        put_out(ENC_OUT, half, dot_tn((kc, vc)[half][...], gl[...]))
    weight_grad(ENC + 3, o[...], dq[...])
    net.tick(AT_ENC_FFN_GRADS, 0)
    halves = [(start, size, patches) for start, size in wide_tiles]
    attend_back(
        q, k, v, lse, do, dq, dk, dv, dk_acc, dv_acc, halves, None, net.ticks(AT_ENC_BACK)
    )
    net.tick(AT_ENC_END, 0)
    weight_grad(ENC, xl[...], dq[...])
    weight_grad(ENC + 1, xl[...], dk[...])
    weight_grad(ENC + 2, xl[...], dv[...])
    net.tick(AT_ENC_GRADS, 0)
    for number, (start, size) in enumerate(wide_tiles):
        rows = pl.ds(start, size)
        grad = (
            dm[rows, :]
            + dot_nt(dq[rows, :], whole(ENC))
            + dot_nt(dk[rows, :], whole(ENC + 1))
            + dot_nt(dv[rows, :], whole(ENC + 2))
        )
        projected = dot_nt(feat[rows, :], project)
        count_up(AFFINE, grad * (projected - row(BN)) * bn_scale)
        count_up(AFFINE + 1, grad)
        low = (grad * (bn_scale * row(AFFINE))).astype(LOW)
        gl[rows, :] = low
        r2[rows, 0:channels] = dot_nn(low, project)
        net.tick(AT_PROJECT_BACK, number)
    out = pltpu.make_async_copy(r2.at[:, 0:channels], gfeat, done)
    out.start()
    columns = gvec[...].T
    lane = lax.broadcasted_iota(jnp.int32, columns.shape, 1)
    for index, first in ((0, ENC_HIDDEN), (1, DEC_HIDDEN)):
        for i, column in enumerate(bias_columns(gbias[index : index + 1, :])):
            columns = jnp.where(lane == first + i, column, columns)
    put(
        MISC,
        None,
        jnp.concatenate(
            [
                dot_tn(gl[...], feat[...]),
                columns,
                jnp.zeros((width, width - channels - VECTOR_ROWS), WIDE),
            ],
            axis=1,
        ),
    )
    net.flush()
    out.wait()


def math_buffers(patches, tags, width, hidden):
    wide = lambda *shape: pltpu.VMEM(shape, WIDE)
    low = lambda *shape: pltpu.VMEM(shape, LOW)
    rows, slots = (patches, width), (tags, width)
    return [
        wide(*rows), low(*rows), low(*rows), low(*rows), low(*rows), low(*rows), wide(patches, 128),
        wide(*rows), low(*rows),
        wide(*slots), low(*slots), low(*slots), low(*slots), low(*slots), low(*slots), wide(tags, 128),
        wide(*slots), low(*slots), low(*slots), low(*rows), low(*rows), low(*slots), wide(tags, 128),
        low(*rows), low(tags, hidden), low(*rows),
        low(*rows), low(*rows), low(*rows), low(*rows), wide(*rows),
        wide(128, patches), wide(128, patches), wide(VECTOR_ROWS, width), wide(VECTOR_ROWS, width),
        wide(8, hidden), pltpu.SemaphoreType.DMA(()),
    ]


class Quiet:
    def tick(self, name, number):
        pass

    def ticks(self, name):
        return ()

    def fence(self, name):
        pass

    def flush(self):
        pass


LAST = 9
HEAD = (
    ((E1, 0),),
    ((E1, 1), (E2, 0)),
    ((E1, 2), (D1, 0)),
    ((E1, 3), (E2, 1)),
)
PLAN = {
    (AT_ENCODE, 1): ((E2, 2), (D2, 0)),
    (AT_ENC_ATTEND, 1): ((D1, 1),),
    (AT_ENC_ATTEND, 2): ((E2, 3), (D3, 0)),
    (AT_ENC_ATTEND, 3): ((D1, 2), (D2, 1)),
    (AT_ENC_FEED, 0): ((D2, 2), (D3, 1)),
    (AT_ENC_FEED, 1): ((D1, 3),),
    (AT_SELF_ATTEND, 4): ((D3, 2),),
    (AT_SELF_ATTEND, 7): ((D2, 3),),
    (AT_CROSS_ATTEND, 2): ((D3, 3), (D2, LAST)),
    (AT_DEC_FEED, 1): ((D3, LAST),),
    (AT_DEC_FFN_GRADS, 0): ((RD3, 0),),
    (AT_CROSS_BACK, 1): ((RD3, 1),),
    (AT_CROSS_END, 0): ((RD3, 2), (D1, LAST)),
    (AT_CROSS_GRADS, 0): ((RD3, 3), (RD2, 0)),
    (AT_SELF_BACK, 4): ((RD2, 1),),
    (AT_SELF_END, 0): ((RD3, 4),),
    (AT_SELF_GRADS, 0): ((RD1, 0),),
    (AT_ENC_FEED_BACK, 0): ((RD2, 2),),
    (AT_ENC_FEED_BACK, 1): ((RD1, 1), (E1, LAST), (E2, LAST)),
    (AT_ENC_FFN_GRADS, 0): ((RD2, 3), (RE2, 0)),
    (AT_ENC_BACK, 2): ((RD1, 2),),
    (AT_ENC_BACK, 3): ((RD2, 4), (RE2, 1)),
    (AT_ENC_BACK, 4): ((RD1, 3),),
    (AT_ENC_BACK, 6): ((RE2, 2),),
    (AT_ENC_BACK, 7): ((RD1, 4),),
    (AT_ENC_END, 0): ((RE2, 3),),
    (AT_ENC_GRADS, 0): ((RA, 0),),
    (AT_PROJECT_BACK, 1): ((RE2, 4), (RA, 1)),
}
TAIL = (
    ((RB, 0),),
    ((RA, 2), (RB, 1)),
    ((RA, 3), (RB, 2)),
    ((RA, 4), (RB, 3)),
    ((RB, 4),),
)
GATHERS = {
    E1: ((MISC, 2, 0), (MISC + 2, 2, 1)),
    E2: ((ENC + 3, 3, 0), (ENC + 6, 2, 1)),
    D1: ((SELF, 2, 0), (SELF + 2, 2, 1)),
    D2: ((CROSS, 2, 0), (CROSS + 2, 2, 1)),
    D3: ((DEC_IN, 2, 0), (DEC_OUT, 2, 1)),
}
SCATTERS = {
    RD3: ((DEC_IN, DEC_IN, 2, 0, 0, 0), (DEC_OUT, DEC_OUT, 2, 1, 1, 0)),
    RD2: ((CROSS, CROSS, 2, 0, 2, 0), (CROSS + 2, CROSS + 2, 2, 1, 3, 0)),
    RD1: ((SELF, SELF, 2, 0, 4, 0), (SELF + 2, SELF + 2, 2, 1, 5, 0)),
    RE2: ((ENC + 3, ENC + 3, 3, 0, 0, 0), (ENC + 6, ENC + 6, 2, 1, 1, 0)),
    RA: ((SELF, ENC, 2, 0, 2, 0), (SELF + 2, ENC + 2, 1, 1, 3, 0)),
    RB: ((MISC, MISC, 1, 1, 3, 1),),
}
INBOX = (3, 2, 2, 2, 2, 2)


class Traffic:
    def __init__(self, place, w, inboxes, share, sems):
        gather_out, gather_in, scatter_out, scatter_in = sems
        self.groups, base = {}, 0
        for name, runs in GATHERS.items():
            self.groups[name] = Group([])
            for first, count, route in runs:
                pieces = (first, first + count)
                self.groups[name].runs.append(
                    Gather(w, place, pieces, ROUTES[route], gather_out, gather_in, base)
                )
                base += Gather.sems
        base = 0
        for name, runs in SCATTERS.items():
            self.groups[name] = Group([])
            for slot, piece, count, route, inbox, room in runs:
                self.groups[name].runs.append(
                    Scatter(
                        w, place, (slot, slot + count), ROUTES[route], inboxes[inbox], room, share, piece,
                        scatter_out, scatter_in, base,
                    )
                )
                base += Scatter.sems

    def run(self, steps):
        for name, step in steps:
            if step == LAST:
                self.groups[name].drain()
            else:
                self.groups[name].advance(step)

    def tick(self, name, number):
        self.run(PLAN.get((name, number), ()))

    def ticks(self, name):
        plans = [PLAN.get((name, number)) for number in range(HEADS)]
        return tuple(partial(self.run, plan) if plan else None for plan in plans)

    def fence(self, name):
        self.groups[name].finish()

    def flush(self):
        for plan in TAIL:
            self.run(plan)


POS_AT = 7


def fused_kernel(
    feat, ids, lens, cot, pos, proj, bn_given, bn_affine, enc_attn, enc_vec, enc_in, enc_hidden, enc_out,
    table, dec_self, dec_cross, dec_vec, dec_in, dec_hidden, dec_out, decoded, gfeat, share, *scratch
):
    w, cols, turned = scratch[:3]
    boxes = 3 + 4 * len(INBOX)
    inboxes = [scratch[3 + 4 * i : 7 + 4 * i] for i in range(len(INBOX))]
    sems, bufs = scratch[boxes : boxes + 5], scratch[boxes + 5 :]
    place = my_place()
    greet(place)
    width = w.shape[-1]
    rows = w.shape[-2]
    local = sems[0]
    channels = proj.shape[1]

    def own(first, count=1):
        return cube(w, (first, first + count), place, ())

    copies = [(enc_attn, own(ENC, 4)), (dec_self, own(SELF, 4)), (dec_cross, own(CROSS, 4))]
    for matrix, first in ((enc_in, ENC_IN), (dec_in, DEC_IN)):
        copies += [
            (matrix.at[:, half * width : (half + 1) * width], own(first + half).at[0])
            for half in range(2)
        ]
    for matrix, first in ((enc_out, ENC_OUT), (dec_out, DEC_OUT)):
        copies += [
            (matrix.at[half * rows : (half + 1) * rows, :], own(first + half).at[0])
            for half in range(2)
        ]
    copies = [
        pltpu.make_async_copy(source, target, local.at[number])
        for number, (source, target) in enumerate(copies)
    ]
    for copy in copies:
        copy.start()
    fetch = pltpu.make_async_copy(pos, bufs[-POS_AT], local.at[11])
    fetch.start()
    cols[...] = jnp.zeros_like(cols)
    for part, first in ((bn_given, BN), (bn_affine, AFFINE), (enc_vec, ENC_VEC), (dec_vec, DEC_VEC)):
        cols[first : first + part.shape[0], 0:rows] = part[...].astype(WIDE)
    for part, first in ((enc_hidden, ENC_HIDDEN), (dec_hidden, DEC_HIDDEN)):
        for half in range(2):
            cols[first + half : first + half + 1, 0:rows] = part[0:1, half * rows : (half + 1) * rows].astype(WIDE)
    turned[...] = cols[...].T[0:rows, :]
    turned[:, TABLE : TABLE + VOCAB] = table[...].astype(WIDE)
    first = jnp.concatenate(
        [proj[...], turned[...].astype(LOW), jnp.zeros((rows, width - channels - VECTOR_ROWS), LOW)], axis=1
    )
    own(MISC)[...] = first[None]
    await_greetings()
    for copy in copies:
        copy.wait()
    net = Traffic(place, w, inboxes, share, sems[1:])
    for plan in HEAD:
        net.run(plan)

    def put(piece, half, value):
        slot = piece - ENC + SELF if ENC <= piece < ENC + 3 else piece
        if half is None:
            w[slot] = value.reshape(BITS + (rows, width)).astype(LOW)
        else:
            w[slot, half] = value.reshape(BITS[1:] + (rows, width)).astype(LOW)

    fetch.wait()
    layer_math(feat, ids, lens[0], cot, w, decoded, gfeat, put, net, bufs)


def plain_kernel(feat, ids, lens, cot, pos, w, decoded, gfeat, g, *bufs):
    width = w.shape[-1]

    def put(piece, half, value):
        if half is None:
            g[piece] = value.reshape(g.shape[1:]).astype(LOW)
        else:
            g[piece, half] = value.reshape(g.shape[2:]).astype(LOW)

    pltpu.sync_copy(pos, bufs[-POS_AT])
    layer_math(feat, ids, lens[0], cot, w, decoded, gfeat, put, Quiet(), bufs)


VMEM = pl.BlockSpec(memory_space=pltpu.VMEM)
SMEM = pl.BlockSpec(memory_space=pltpu.SMEM)
ANY = pl.BlockSpec(memory_space=pl.ANY)
LIMIT = 63 << 20


def split_update(features, tag_ids, tag_lengths, out_cot, parameters):
    (
        proj, bn_given, bn_affine, enc_attn, enc_vec, enc_in, enc_hidden, enc_out,
        table, dec_self, dec_cross, dec_vec, dec_in, dec_hidden, dec_out,
    ) = parameters
    patches, channels = features.shape[1:]
    tags, width = out_cot.shape[1:]
    rows = width // BLOCKS
    pos = jnp.asarray(position_table(max(patches, tags), width))
    sems = (
        Gather.sems * sum(len(runs) for runs in GATHERS.values()),
        Scatter.sems * sum(len(runs) for runs in SCATTERS.values()),
    )
    boxes = [
        pltpu.VMEM(shape, LOW)
        for number, count in enumerate(INBOX)
        for shape in inbox_shapes(count, ROUTES[number % 2], rows, width)
    ]
    dma = pltpu.SemaphoreType.DMA
    decoded, gfeat, share = pl.pallas_call(
        fused_kernel,
        in_specs=[VMEM, VMEM, SMEM, VMEM, ANY, VMEM, VMEM, VMEM, ANY, VMEM, ANY, VMEM, ANY]
        + [VMEM, ANY, ANY, VMEM, ANY, VMEM, ANY],
        out_shape=(
            jax.ShapeDtypeStruct((tags, width), LOW),
            jax.ShapeDtypeStruct((patches, channels), WIDE),
            jax.ShapeDtypeStruct((PIECES, rows, width), WIDE),
        ),
        out_specs=(VMEM, ANY, VMEM),
        scratch_shapes=[
            pltpu.VMEM((PIECES,) + BITS + (rows, width), LOW),
            pltpu.VMEM((VECTOR_ROWS, 128), WIDE),
            pltpu.VMEM((rows, VECTOR_ROWS), WIDE),
            *boxes,
            dma((12,)),
            dma((sems[0],)),
            dma((sems[0],)),
            dma((sems[1],)),
            dma((sems[1],)),
            *math_buffers(patches, tags, width, enc_in.shape[1]),
        ],
        compiler_params=pltpu.CompilerParams(
            collective_id=0, has_side_effects=True, vmem_limit_bytes=LIMIT
        ),
        name="layers",
    )(
        features[0], tag_ids, tag_lengths, out_cot[0], pos, proj.T, bn_given, bn_affine, enc_attn, enc_vec,
        enc_in, enc_hidden.reshape(1, -1), enc_out, table.T, dec_self, dec_cross, dec_vec, dec_in,
        dec_hidden.reshape(1, -1), dec_out,
    )
    outs = finish(decoded, gfeat, share, channels)
    return (
        outs[0][None],
        outs[1][None],
        outs[2].T,
        *outs[3:7],
        outs[7].reshape(-1),
        outs[8],
        outs[9].T,
        *outs[10:14],
        outs[14].reshape(-1),
        outs[15],
    )


def finish_kernel(
    decoded, gfeat, share, decoded_out, gfeat_out, proj, affine, enc_attn, enc_vec, enc_in, enc_hidden,
    enc_out, table, dec_self, dec_cross, dec_vec, dec_in, dec_hidden, dec_out
):
    rows, width = share.shape[1:]
    channels = proj.shape[1]
    decoded_out[...] = decoded[...]
    gfeat_out[...] = gfeat[...]
    enc_attn[...] = share[ENC : ENC + 4]
    dec_self[...] = share[SELF : SELF + 4]
    dec_cross[...] = share[CROSS : CROSS + 4]
    for half in range(2):
        enc_in[:, half * width : (half + 1) * width] = share[ENC_IN + half]
        dec_in[:, half * width : (half + 1) * width] = share[DEC_IN + half]
        enc_out[half * rows : (half + 1) * rows, :] = share[ENC_OUT + half]
        dec_out[half * rows : (half + 1) * rows, :] = share[DEC_OUT + half]
    columns = share[MISC]
    proj[...] = columns[:, 0:channels]
    table[...] = columns[:, channels + TABLE : channels + TABLE + VOCAB]
    vectors = jnp.concatenate(
        [columns[:, channels : channels + VECTOR_ROWS], jnp.zeros((128 - rows, VECTOR_ROWS), WIDE)],
        axis=0,
    ).T[:, 0:rows]
    for part, first in ((affine, AFFINE), (enc_vec, ENC_VEC), (dec_vec, DEC_VEC)):
        part[...] = vectors[first : first + part.shape[0]]
    for part, first in ((enc_hidden, ENC_HIDDEN), (dec_hidden, DEC_HIDDEN)):
        part[...] = jnp.concatenate([vectors[first : first + 1], vectors[first + 1 : first + 2]], axis=1)


def finish(decoded, gfeat, share, channels):
    rows, width = share.shape[1:]
    shape = lambda *dims: jax.ShapeDtypeStruct(dims, WIDE)
    return pl.pallas_call(
        finish_kernel,
        in_specs=[VMEM] * 3,
        out_shape=(
            jax.ShapeDtypeStruct(decoded.shape, decoded.dtype),
            jax.ShapeDtypeStruct(gfeat.shape, gfeat.dtype),
            shape(rows, channels),
            shape(2, rows),
            shape(4, rows, width),
            shape(5, rows),
            shape(rows, 2 * width),
            shape(1, 2 * rows),
            shape(2 * rows, width),
            shape(rows, VOCAB),
            shape(4, rows, width),
            shape(4, rows, width),
            shape(7, rows),
            shape(rows, 2 * width),
            shape(1, 2 * rows),
            shape(2 * rows, width),
        ),
        out_specs=(VMEM,) * 16,
        name="finish",
    )(decoded, gfeat, share)


def gathered_update(features, tag_ids, tag_lengths, out_cot, parameters):
    dims = (1, 1, 1, 1, 1, 0, 0, 0, 1, 1, 1, 1, 0, 0, 0)
    full = [lax.all_gather(a, AXES, axis=d, tiled=True) for a, d in zip(parameters, dims)]
    (
        proj, bn_given, bn_affine, enc_attn, enc_vec, enc_in, enc_hidden, enc_out,
        table, dec_self, dec_cross, dec_vec, dec_in, dec_hidden, dec_out,
    ) = full
    patches, channels = features.shape[1:]
    tags, width = out_cot.shape[1:]
    rows = width // BLOCKS

    def swap(matrix):
        return matrix.reshape((BLOCKS, 2, -1) + matrix.shape[1:]).swapaxes(0, 1).reshape((2, -1) + matrix.shape[1:])

    def halves(matrix):
        return jnp.stack([matrix[:, :width], matrix[:, width:]])

    columns = jnp.concatenate(
        [proj, bn_given, bn_affine, enc_vec, dec_vec, table, swap(enc_hidden), swap(dec_hidden)], axis=0
    )
    columns = jnp.pad(columns, ((0, width - columns.shape[0]), (0, 0))).T
    stack = jnp.concatenate(
        [columns[None], enc_attn, halves(enc_in), swap(enc_out), dec_self, dec_cross]
        + [halves(dec_in), swap(dec_out)],
        axis=0,
    ).reshape((PIECES,) + BITS + (rows, width))
    decoded, gfeat, grads = pl.pallas_call(
        plain_kernel,
        in_specs=[VMEM, VMEM, SMEM, VMEM, ANY, VMEM],
        out_shape=(
            jax.ShapeDtypeStruct((tags, width), LOW),
            jax.ShapeDtypeStruct((patches, channels), WIDE),
            jax.ShapeDtypeStruct(stack.shape, LOW),
        ),
        out_specs=(VMEM, ANY, VMEM),
        scratch_shapes=math_buffers(patches, tags, width, enc_in.shape[1]),
        compiler_params=pltpu.CompilerParams(vmem_limit_bytes=LIMIT),
        name="layers",
    )(features[0], tag_ids, tag_lengths, out_cot[0], jnp.asarray(position_table(max(patches, tags), width)), stack)
    grads = grads.reshape(PIECES, width, width).astype(WIDE)
    columns = grads[MISC].T
    vectors = columns[channels:]

    def join(pair):
        return pair.reshape((2, BLOCKS, -1) + pair.shape[2:]).swapaxes(0, 1).reshape((-1,) + pair.shape[2:])

    def wide(pair):
        return jnp.concatenate([pair[0], pair[1]], axis=1)

    totals = (
        (columns[:channels], 1),
        (vectors[AFFINE : AFFINE + 2], 1),
        (grads[ENC : ENC + 4], 1),
        (vectors[ENC_VEC:DEC_VEC], 1),
        (wide(grads[ENC_IN:ENC_OUT]), 0),
        (join(vectors[ENC_HIDDEN : ENC_HIDDEN + 2]), 0),
        (join(grads[ENC_OUT:SELF]), 0),
        (vectors[TABLE : TABLE + VOCAB], 1),
        (grads[SELF:CROSS], 1),
        (grads[CROSS:DEC_IN], 1),
        (vectors[DEC_VEC:TABLE], 1),
        (wide(grads[DEC_IN:DEC_OUT]), 0),
        (join(vectors[DEC_HIDDEN : DEC_HIDDEN + 2]), 0),
        (join(grads[DEC_OUT:PIECES]), 0),
    )
    return (
        decoded[None],
        gfeat[None],
        *[lax.psum_scatter(a, AXES, scatter_dimension=d, tiled=True) for a, d in totals],
    )


def body(mesh_shape, features, tag_ids, tag_lengths, out_cot, *parameters):
    update = split_update if mesh_shape == (16, 2) else gathered_update
    return update(features, tag_ids, tag_lengths, out_cot, parameters)


def solution(mesh):
    placed = (
        P(("wide", "narrow"), None, None),
        P(("wide", "narrow"), None),
        P(("wide", "narrow")),
        P(("wide", "narrow"), None, None),
        P(None, ("wide", "narrow")),
        P(None, ("wide", "narrow")),
        P(None, ("wide", "narrow")),
        P(None, ("wide", "narrow"), None),
        P(None, ("wide", "narrow")),
        P(("wide", "narrow"), None),
        P(("wide", "narrow")),
        P(("wide", "narrow"), None),
        P(None, ("wide", "narrow")),
        P(None, ("wide", "narrow"), None),
        P(None, ("wide", "narrow"), None),
        P(None, ("wide", "narrow")),
        P(("wide", "narrow"), None),
        P(("wide", "narrow")),
        P(("wide", "narrow"), None),
    )
    return jax.shard_map(
        partial(body, tuple(mesh.shape[axis] for axis in AXES)),
        mesh=mesh,
        in_specs=placed,
        out_specs=(
            P(("wide", "narrow"), None, None),
            P(("wide", "narrow"), None, None),
            P(None, ("wide", "narrow")),
            P(None, ("wide", "narrow")),
            P(None, ("wide", "narrow"), None),
            P(None, ("wide", "narrow")),
            P(("wide", "narrow"), None),
            P(("wide", "narrow")),
            P(("wide", "narrow"), None),
            P(None, ("wide", "narrow")),
            P(None, ("wide", "narrow"), None),
            P(None, ("wide", "narrow"), None),
            P(None, ("wide", "narrow")),
            P(("wide", "narrow"), None),
            P(("wide", "narrow")),
            P(("wide", "narrow"), None),
        ),
        check_vma=False,
    )
```

```python
from functools import partial
import math

import jax
import jax.numpy as jnp
import numpy as np
from jax import lax
from jax.experimental import pallas as pl
from jax.experimental.pallas import tpu as pltpu
from jax.sharding import PartitionSpec as P

HEADS = 8
VOCAB = 32
AXES = ("wide", "narrow")
LOW = jnp.bfloat16
WIDE = jnp.float32

MISC, ENC, ENC_IN, ENC_OUT, SELF, CROSS, DEC_IN, DEC_OUT, PIECES = 0, 1, 5, 7, 9, 13, 17, 19, 21
BITS = (2,) * 5
BLOCKS = 32
BN, AFFINE, ENC_VEC, DEC_VEC, TABLE, VECTOR_ROWS = 0, 2, 4, 9, 16, 128
E1, E2, D1, D2, D3, RD3, RD2, RD1, RE2, RA, RB = range(11)
(
    AT_ENCODE,
    AT_ENC_ATTEND,
    AT_ENC_FEED,
    AT_SELF_ATTEND,
    AT_CROSS_ATTEND,
    AT_DEC_FEED,
    AT_DEC_FFN_GRADS,
    AT_CROSS_BACK,
    AT_CROSS_END,
    AT_SELF_ROWS,
    AT_CROSS_GRADS,
    AT_SELF_BACK,
    AT_SELF_END,
    AT_SELF_GRADS,
    AT_ENC_FEED_BACK,
    AT_ENC_FFN_GRADS,
    AT_ENC_BACK,
    AT_ENC_END,
    AT_ENC_GRADS,
    AT_PROJECT_BACK,
    AT_DECODE,
) = range(21)
ENC_HIDDEN, DEC_HIDDEN = TABLE + VOCAB, TABLE + VOCAB + 2


def dot_nn(left, right):
    return lax.dot_general(left, right, (((1,), (0,)), ((), ())), preferred_element_type=WIDE)


def dot_nt(left, right):
    return lax.dot_general(left, right, (((1,), (1,)), ((), ())), preferred_element_type=WIDE)


def dot_tn(left, right):
    return lax.dot_general(left, right, (((0,), (0,)), ((), ())), preferred_element_type=WIDE)


def position_table(rows, width):
    place = np.arange(rows, dtype=np.float64)[:, None]
    column = np.arange(width)
    inverse = np.exp(-(2 * (column // 2)) / width * math.log(10000.0))
    angle = place * inverse[None, :]
    return np.where((column % 2 == 0)[None, :], np.sin(angle), np.cos(angle)).astype(np.float32)


def norm_stats(value):
    centred = value - jnp.mean(value, axis=1, keepdims=True)
    scale = lax.rsqrt(jnp.mean(centred * centred, axis=1, keepdims=True) + 1e-05)
    return centred * scale, scale


def norm_back(grad, normal, scale, gain):
    inner = grad * gain
    return scale * (
        inner
        - jnp.mean(inner, axis=1, keepdims=True)
        - normal * jnp.mean(inner * normal, axis=1, keepdims=True)
    )


def col_sum(value):
    return jnp.sum(value, axis=0, keepdims=True)


def gauss_share(value):
    return 0.5 + 0.5 * lax.erf(value * math.sqrt(0.5))


def gauss_slope(value):
    return jnp.exp(value * value * -0.5) * (1.0 / math.sqrt(2.0 * math.pi))


def two_tiles(count):
    top = (count // 2 + 15) // 16 * 16
    return [(0, top), (top, count - top)]


def pick(mask, half, value):
    zero = jnp.zeros((), value.dtype)
    return jnp.where(mask, value, zero) if half == 0 else jnp.where(mask, zero, value)


def first_half(shape):
    return lax.broadcasted_iota(jnp.int32, shape, 1) < shape[1] // 2


FAR, NEAR, SIDE, CORE, ACROSS = range(5)
DEEP = (FAR, NEAR)
ROUTES = ((DEEP, (ACROSS,), (SIDE,)), (DEEP, (SIDE,), (ACROSS,)), ((ACROSS,), (SIDE,), DEEP))


def my_place():
    wide = lax.axis_index("wide")
    return (wide // 8, wide // 4 % 2, wide // 2 % 2, wide % 2, lax.axis_index("narrow"))


def flips(axes):
    if len(axes) == 1:
        return [axes]
    return [axes[:1], axes[1:], axes]


def across(place, flip):
    return tuple(1 - p if i in flip else p for i, p in enumerate(place))


def device_at(place):
    far, near, side, core, narrow = place
    return (far * 8 + near * 4 + side * 2 + core, narrow)


def greet(place):
    for flip in flips(DEEP) + [(SIDE,), (CORE,), (ACROSS,)]:
        pl.semaphore_signal(
            pltpu.get_barrier_semaphore(),
            inc=1,
            device_id=device_at(across(place, flip)),
            device_id_type=pl.DeviceIdType.MESH,
        )


def await_greetings():
    pl.semaphore_wait(pltpu.get_barrier_semaphore(), 6)


def cube(stack, pieces, place, open_axes):
    index = tuple(slice(None) if i in open_axes else p for i, p in enumerate(place))
    return stack.at[(slice(*pieces),) + index]


class Gather:
    sems = 8

    def __init__(self, stack, place, pieces, route, sends, arrivals, base):
        self.stack, self.place, self.pieces, self.route = stack, place, pieces, route
        self.sends, self.arrivals, self.base = sends, arrivals, base

    def copy(self, which, flip, place, open_axes):
        part = cube(self.stack, self.pieces, place, open_axes)
        return pltpu.make_async_remote_copy(
            src_ref=part,
            dst_ref=part,
            send_sem=self.sends.at[self.base + which],
            recv_sem=self.arrivals.at[self.base + which],
            device_id=device_at(across(self.place, flip)),
            device_id_type=pl.DeviceIdType.MESH,
        )

    def hop(self, step):
        before = self.route[:step]
        first = sum(len(flips(axes)) for axes in before)
        held = sum(before, ())
        return [
            self.copy(first + i, flip, self.place, held)
            for i, flip in enumerate(flips(self.route[step]))
        ]

    def hand(self, last):
        held = self.route[0] + self.route[1]
        if not last:
            return [self.copy(4 + len(flips(self.route[2])), (CORE,), self.place, held)]
        return [
            self.copy(5 + len(flips(self.route[2])) + i, (CORE,), across(self.place, flip), held)
            for i, flip in enumerate(flips(self.route[2]))
        ]

    def advance(self, step):
        if step:
            for copy in self.hop(step - 1):
                copy.wait_recv()
        if step < 3:
            for copy in self.hop(step):
                copy.start()
        if step >= 2:
            for copy in self.hand(step == 3):
                copy.start()

    def finish(self):
        for copy in self.hand(False) + self.hand(True):
            copy.wait_recv()

    def drain(self):
        for copy in sum([self.hop(step) for step in range(3)], []) + self.hand(False) + self.hand(True):
            copy.wait_send()


class Scatter:
    sems = 6

    def __init__(self, stack, place, slots, route, inbox, room, share, piece, sends, arrivals, base):
        self.stack, self.place, self.slots, self.piece = stack, place, slots, piece
        self.order = ((CORE,),) + tuple(reversed(route))
        self.inbox, self.room, self.share = inbox, room, share
        self.sends, self.arrivals, self.base = sends, arrivals, base

    def open_axes(self, step):
        return [a for a in range(5) if a not in sum(self.order[: step + 1], ())]

    def hop(self, step):
        first = sum(len(flips(axes)) for axes in self.order[:step])
        count = self.slots[1] - self.slots[0]
        return [
            pltpu.make_async_remote_copy(
                src_ref=cube(self.stack, self.slots, across(self.place, flip), self.open_axes(step)),
                dst_ref=self.inbox[step].at[i, self.room : self.room + count],
                send_sem=self.sends.at[self.base + first + i],
                recv_sem=self.arrivals.at[self.base + first + i],
                device_id=device_at(across(self.place, flip)),
                device_id_type=pl.DeviceIdType.MESH,
            )
            for i, flip in enumerate(flips(self.order[step]))
        ]

    def advance(self, step):
        if step:
            for copy in self.hop(step - 1):
                copy.wait_recv()
            self.add(step - 1)
        if step < 4:
            for copy in self.hop(step):
                copy.start()
        else:
            self.drain()

    def add(self, step):
        first = self.slots[0]
        for at in range(self.slots[1] - first):
            mine = cube(self.stack, (first + at, first + at + 1), self.place, self.open_axes(step))
            if step < 3 and len(flips(self.order[step])) == 1:
                mine[...] = mine[...] + self.inbox[step][0, self.room + at][None]
                continue
            total = mine[...][0].astype(WIDE)
            for i in range(len(flips(self.order[step]))):
                total = total + self.inbox[step][i, self.room + at].astype(WIDE)
            if step < 3:
                mine[...] = total.astype(mine.dtype)[None]
            else:
                self.share[self.piece + at] = total

    def drain(self):
        for step in range(4):
            for copy in self.hop(step):
                copy.wait_send()


def inbox_shapes(count, route, rows, width):
    order, left, shapes = ((CORE,),) + tuple(reversed(route)), 5, []
    for axes in order:
        left -= len(axes)
        shapes.append((len(flips(axes)), count) + (2,) * left + (rows, width))
    return shapes


class Group:
    def __init__(self, runs):
        self.runs = runs

    def advance(self, step):
        for run in self.runs:
            run.advance(step)

    def finish(self):
        for run in self.runs:
            run.finish()

    def drain(self):
        for run in self.runs:
            run.drain()


def run_tick(index, ticks):
    for at, tick in enumerate(ticks):
        if tick is not None:
            pl.when(index == at)(tick)


def pair_ticks(ticks, number, count):
    return ticks[number::count]


def attend(q_ref, k_ref, v_ref, o_ref, lse_ref, tiles, length, ticks=()):
    slab = 128
    half_scale = LOW(0.125)

    def pair(index, _):
        cols = pl.ds(pl.multiple_of(index * slab, slab), slab)
        for number, (start, size, keys) in enumerate(tiles):
            run_tick(index, pair_ticks(ticks, number, len(tiles)))
            rows = pl.ds(start, size)
            k = k_ref[0:keys, cols]
            v = v_ref[0:keys, cols]
            left_k = first_half(v.shape)
            q = q_ref[rows, cols] * half_scale
            left = first_half(q.shape)
            outs, tops, sums = [], [], []
            for half in range(2):
                s = dot_nt(pick(left, half, q), k)
                if length is not None:
                    s = mask_scores(s, start, length)
                top = jnp.max(s, axis=1, keepdims=True)
                p = jnp.exp(s - top).astype(LOW)
                ones = jnp.ones((), LOW)
                full = jnp.where(left_k, v, ones) if half == 0 else jnp.where(left_k, ones, v)
                out = dot_nn(p, full)
                outs.append(out)
                tops.append(top)
                sums.append(out[:, 64:65] if half == 0 else out[:, 0:1])
            o_ref[rows, cols] = jnp.where(left, outs[0] / sums[0], outs[1] / sums[1]).astype(LOW)
            lane = lax.broadcasted_iota(jnp.int32, (size, slab), 1) - 2 * index
            kept = jnp.where(lane == 0, tops[0] + jnp.log(sums[0]), lse_ref[rows, :])
            lse_ref[rows, :] = jnp.where(lane == 1, tops[1] + jnp.log(sums[1]), kept)
        return 0

    lax.fori_loop(0, HEADS // 2, pair, 0)


def mask_scores(s, start, length):
    query = lax.broadcasted_iota(jnp.int32, s.shape, 0) + start
    key = lax.broadcasted_iota(jnp.int32, s.shape, 1)
    return jnp.where((key <= query) & (key < length), s, -1e30)


def attend_back(
    q_ref, k_ref, v_ref, lse_ref, do_ref, dq_ref, dk_ref, dv_ref, dk_acc, dv_acc, tiles, length, ticks=()
):
    slab = 128
    half_scale = LOW(0.125)
    total = k_ref.shape[0]

    def pair(index, _):
        cols = pl.ds(pl.multiple_of(index * slab, slab), slab)
        first = True
        for number, (start, size, keys) in enumerate(sorted(tiles, key=lambda t: -t[2])):
            run_tick(index, pair_ticks(ticks, number, len(tiles)))
            rows = pl.ds(start, size)
            k = k_ref[0:keys, cols]
            v = v_ref[0:keys, cols]
            q = q_ref[rows, cols] * half_scale
            do = do_ref[rows, cols]
            lane = lax.broadcasted_iota(jnp.int32, (size, slab), 1) - 2 * index
            left = first_half(q.shape)
            grads, dks, dvs = [], [], []
            for half in range(2):
                qh, doh = pick(left, half, q), pick(left, half, do)
                s = dot_nt(qh, k)
                if length is not None:
                    s = mask_scores(s, start, length)
                lse = jnp.sum(jnp.where(lane == half, lse_ref[rows, :], 0.0), axis=1, keepdims=True)
                p = jnp.exp(s - lse)
                mixed = p * dot_nt(doh, v)
                ds = (mixed - p * jnp.sum(mixed, axis=1, keepdims=True)).astype(LOW)
                p = p.astype(LOW)
                grads.append(dot_nn(ds, k))
                dks.append(dot_tn(qh, ds))
                dvs.append(dot_tn(doh, p))
            dq_ref[rows, cols] = (jnp.where(left, grads[0], grads[1]) * 0.125).astype(LOW)
            if first:
                dk_acc[:, 0:keys] = dks[0] + dks[1]
                dv_acc[:, 0:keys] = dvs[0] + dvs[1]
            else:
                dk_acc[:, 0:keys] += dks[0] + dks[1]
                dv_acc[:, 0:keys] += dvs[0] + dvs[1]
            first = False
        dk_ref[0:total, cols] = dk_acc[:, 0:total].T.astype(LOW)
        dv_ref[0:total, cols] = dv_acc[:, 0:total].T.astype(LOW)
        return 0

    lax.fori_loop(0, HEADS // 2, pair, 0)


def layer_math(feat, ids, length, cot, w, decoded, gfeat, put, net, bufs):
    (
        x, xl, q, k, v, o, lse, r2, ml, e, el, qs, ks, vs, os, lses, s2, sl, qc, kc, vc, oc, lsec,
        fl, hid, gl, do, dq, dk, dv, dm, dk_acc, dv_acc, vec, gvec, gbias, done,
    ) = bufs
    patches, width = x.shape
    tags = e.shape[0]
    channels = feat.shape[1]
    wide_tiles = two_tiles(patches)
    tag_tiles = two_tiles(tags)
    tag_rows = slice(0, tags)

    def whole(piece):
        return w[piece].reshape(width, width)

    def out_half(piece, half):
        first, second = (w[piece + i, half].reshape(16, 16, width) for i in range(2))
        return jnp.stack([first, second], axis=1).reshape(width, width)

    def put_out(piece, half, value):
        value = value.reshape((2,) * 4 + (2, 16, width))
        for i in range(2):
            put(piece + i, half, value[:, :, :, :, i])

    def row(index):
        return vec[index : index + 1, :]

    def same(shape, left, right):
        at = [lax.broadcasted_iota(jnp.int32, shape, axis) for axis in range(2)]
        return jnp.where(left(at[0]) == right(at[1]), 1.0, 0.0).astype(LOW)

    block_of = same((width, BLOCKS), lambda r: r // 16, lambda d: d)
    quarters = [same((8, BLOCKS), lambda g, i=i: 4 * g + i, lambda d: d) for i in range(4)]
    spots = [same((BLOCKS, 128), lambda u, i=i: 32 * i + u, lambda lane: lane) for i in range(4)]

    def natural_bias(columns, first):
        r = lax.broadcasted_iota(jnp.int32, (width, BLOCKS), 0)
        u = lax.broadcasted_iota(jnp.int32, (width, BLOCKS), 1)
        own = jnp.where(u < 16, columns[:, first : first + 1], columns[:, first + 1 : first + 2])
        blocks = dot_tn(block_of, jnp.where(r % 16 == u % 16, own, 0.0).astype(LOW)).astype(LOW)
        packed = sum(
            dot_nn(dot_nn(quarters[i], blocks).astype(LOW), spots[i]) for i in range(4)
        )
        return [
            jnp.concatenate([packed[4 * half + i : 4 * half + i + 1] for i in range(4)], axis=1)
            for half in range(2)
        ]

    def bias_columns(total):
        packed = jnp.concatenate([total[:, 128 * g : 128 * (g + 1)] for g in range(8)], axis=0)
        columns = 0.0
        for part in range(2):
            low = packed.astype(LOW)
            packed = packed - low.astype(WIDE)
            blocks = sum(
                dot_tn(quarters[i], dot_nt(low, spots[i]).astype(LOW)) for i in range(4)
            )
            columns = columns + dot_nn(block_of, blocks.astype(LOW))
        r = lax.broadcasted_iota(jnp.int32, (width, BLOCKS), 0)
        u = lax.broadcasted_iota(jnp.int32, (width, BLOCKS), 1)
        return [
            jnp.sum(jnp.where(u == r % 16 + 16 * i, columns, 0.0), axis=1, keepdims=True)
            for i in range(2)
        ]

    def count_up(index, value):
        gvec[index : index + 1, :] += col_sum(value)

    net.fence(E1)
    columns = whole(MISC)[:, channels : channels + VECTOR_ROWS].astype(WIDE)
    vec[...] = columns.T
    gvec[...] = jnp.zeros_like(gvec)
    gbias[...] = jnp.zeros_like(gbias)
    enc_bias = natural_bias(columns, ENC_HIDDEN)
    dec_bias = natural_bias(columns, DEC_HIDDEN)
    bn_scale = lax.rsqrt(row(BN + 1) + 1e-05)
    project = whole(MISC)[:, 0:channels]

    for number, (start, size) in enumerate(wide_tiles):
        rows = pl.ds(start, size)
        projected = dot_nt(feat[rows, :], project)
        begin = (projected - row(BN)) * bn_scale * row(AFFINE) + row(AFFINE + 1) + dm[rows, :]
        x[rows, :] = begin
        low = begin.astype(LOW)
        xl[rows, :] = low
        q[rows, :] = dot_nn(low, whole(ENC)).astype(LOW)
        k[rows, :] = dot_nn(low, whole(ENC + 1)).astype(LOW)
        v[rows, :] = dot_nn(low, whole(ENC + 2)).astype(LOW)
        net.tick(AT_ENCODE, number)
    attend(q, k, v, o, lse, [(0, patches, patches)], None, net.ticks(AT_ENC_ATTEND))
    net.fence(D1)

    onehot = (
        lax.broadcasted_iota(jnp.int32, (VOCAB, tags), 0) == ids[0:1, :]
    ).astype(WIDE).astype(LOW)
    table = vec[TABLE : TABLE + VOCAB, :].astype(LOW)
    e[...] = dot_tn(onehot, table) + dm[0:tags, :]
    el[...] = e[...].astype(LOW)
    qs[...] = dot_nn(el[...], whole(SELF)).astype(LOW)
    ks[...] = dot_nn(el[...], whole(SELF + 1)).astype(LOW)
    vs[...] = dot_nn(el[...], whole(SELF + 2)).astype(LOW)
    causal_tiles = [(start, size, start + size) for start, size in tag_tiles]
    attend(qs, ks, vs, os, lses, causal_tiles, length, net.ticks(AT_SELF_ATTEND))
    net.fence(E2)

    for number, (start, size) in enumerate(wide_tiles):
        rows = pl.ds(start, size)
        resid = x[rows, :] + dot_nn(o[rows, :], whole(ENC + 3))
        x[rows, :] = resid
        normal, _scale = norm_stats(resid)
        first = normal * row(ENC_VEC) + row(ENC_VEC + 1)
        low = first.astype(LOW)
        total = first + row(ENC_VEC + 2)
        for half in range(2):
            pre = dot_nn(low, whole(ENC_IN + half)) + enc_bias[half]
            act = (pre * gauss_share(pre)).astype(LOW)
            total = total + dot_nn(act, out_half(ENC_OUT, half))
        r2[rows, :] = total
        normal, _scale = norm_stats(total)
        ml[rows, :] = (normal * row(ENC_VEC + 3) + row(ENC_VEC + 4)).astype(LOW)
        net.tick(AT_ENC_FEED, number)
    net.fence(D2)

    for start, size in tag_tiles:
        rows = pl.ds(start, size)
        resid = e[rows, :] + dot_nn(os[rows, :], whole(SELF + 3))
        e[rows, :] = resid
        normal, _scale = norm_stats(resid)
        second = normal * row(DEC_VEC) + row(DEC_VEC + 1)
        s2[rows, :] = second
        sl[rows, :] = second.astype(LOW)
        qc[rows, :] = dot_nn(sl[rows, :], whole(CROSS)).astype(LOW)
    kc[...] = dot_nn(ml[...], whole(CROSS + 1)).astype(LOW)
    vc[...] = dot_nn(ml[...], whole(CROSS + 2)).astype(LOW)
    net.tick(AT_DECODE, 0)
    attend(qc, kc, vc, oc, lsec, [(0, tags, patches)], None, net.ticks(AT_CROSS_ATTEND))
    net.fence(D3)

    for number, (start, size) in enumerate(tag_tiles):
        rows = pl.ds(start, size)
        resid = s2[rows, :] + dot_nn(oc[rows, :], whole(CROSS + 3))
        normal_two, scale_two = norm_stats(resid)
        third = normal_two * row(DEC_VEC + 2) + row(DEC_VEC + 3)
        low = third.astype(LOW)
        fl[rows, :] = low
        total = third + row(DEC_VEC + 4)
        kept = []
        for half in range(2):
            pre = dot_nn(low, whole(DEC_IN + half)) + dec_bias[half]
            share = gauss_share(pre)
            act = (pre * share).astype(LOW)
            hid[rows, half * width : (half + 1) * width] = act
            total = total + dot_nn(act, out_half(DEC_OUT, half))
            kept.append(share + pre * gauss_slope(pre))
        normal, scale = norm_stats(total)
        place = lax.broadcasted_iota(jnp.int32, (size, 1), 0) + start
        live = jnp.where(place < length, 1.0, 0.0)
        decoded[rows, :] = ((normal * row(DEC_VEC + 5) + row(DEC_VEC + 6)) * live).astype(LOW)
        grad = cot[rows, :].astype(WIDE) * live
        count_up(DEC_VEC + 5, grad * normal)
        count_up(DEC_VEC + 6, grad)
        grad = norm_back(grad, normal, scale, row(DEC_VEC + 5))
        count_up(DEC_VEC + 4, grad)
        grad_low = grad.astype(LOW)
        gl[rows, :] = grad_low
        for half in range(2):
            back = dot_nt(grad_low, out_half(DEC_OUT, half)) * kept[half]
            gbias[1:2, half * width : (half + 1) * width] += col_sum(back)
            back = back.astype(LOW)
            (dk, dv)[half][rows, :] = back
            grad = grad + dot_nt(back, whole(DEC_IN + half))
        count_up(DEC_VEC + 2, grad * normal_two)
        count_up(DEC_VEC + 3, grad)
        grad = norm_back(grad, normal_two, scale_two, row(DEC_VEC + 2))
        s2[rows, :] = grad
        dq[rows, :] = grad.astype(LOW)
        do[rows, :] = dot_nt(dq[rows, :], whole(CROSS + 3)).astype(LOW)
        net.tick(AT_DEC_FEED, number)

    def weight_grad(piece, left, right):
        put(piece, None, dot_tn(left, right))

    for half in range(2):
        cols = slice(half * width, (half + 1) * width)
        weight_grad(DEC_IN + half, fl[tag_rows, :], (dk, dv)[half][tag_rows, :])
        put_out(DEC_OUT, half, dot_tn(hid[tag_rows, cols], gl[tag_rows, :]))
    net.tick(AT_DEC_FFN_GRADS, 0)
    weight_grad(CROSS + 3, oc[...], dq[tag_rows, :])
    attend_back(
        qc, kc, vc, lsec, do, dq, dk, dv, dk_acc, dv_acc, [(0, tags, patches)], None,
        net.ticks(AT_CROSS_BACK),
    )
    net.tick(AT_CROSS_END, 0)
    for start, size in wide_tiles:
        rows = pl.ds(start, size)
        dm[rows, :] = dot_nt(dk[rows, :], whole(CROSS + 1)) + dot_nt(dv[rows, :], whole(CROSS + 2))
    for start, size in tag_tiles:
        rows = pl.ds(start, size)
        grad = s2[rows, :] + dot_nt(dq[rows, :], whole(CROSS))
        normal, scale = norm_stats(e[rows, :])
        count_up(DEC_VEC, grad * normal)
        count_up(DEC_VEC + 1, grad)
        grad = norm_back(grad, normal, scale, row(DEC_VEC))
        s2[rows, :] = grad
        gl[rows, :] = grad.astype(LOW)
        do[rows, :] = dot_nt(gl[rows, :], whole(SELF + 3)).astype(LOW)
    net.tick(AT_SELF_ROWS, 0)
    weight_grad(CROSS, sl[...], dq[tag_rows, :])
    weight_grad(CROSS + 1, ml[...], dk[...])
    weight_grad(CROSS + 2, ml[...], dv[...])
    net.tick(AT_CROSS_GRADS, 0)
    weight_grad(SELF + 3, os[...], gl[tag_rows, :])
    attend_back(
        qs, ks, vs, lses, do, dq, dk, dv, dk_acc, dv_acc, causal_tiles, length,
        net.ticks(AT_SELF_BACK),
    )
    net.tick(AT_SELF_END, 0)
    grad = (
        s2[...]
        + dot_nt(dq[tag_rows, :], whole(SELF))
        + dot_nt(dk[tag_rows, :], whole(SELF + 1))
        + dot_nt(dv[tag_rows, :], whole(SELF + 2))
    )
    high = grad.astype(LOW)
    rest = (grad - high.astype(WIDE)).astype(LOW)
    gvec[TABLE : TABLE + VOCAB, :] = dot_nn(onehot, high) + dot_nn(onehot, rest)
    weight_grad(SELF, el[...], dq[tag_rows, :])
    weight_grad(SELF + 1, el[...], dk[tag_rows, :])
    weight_grad(SELF + 2, el[...], dv[tag_rows, :])
    net.tick(AT_SELF_GRADS, 0)

    for number, (start, size) in enumerate(wide_tiles):
        rows = pl.ds(start, size)
        normal, scale = norm_stats(r2[rows, :])
        grad = dm[rows, :]
        count_up(ENC_VEC + 3, grad * normal)
        count_up(ENC_VEC + 4, grad)
        grad = norm_back(grad, normal, scale, row(ENC_VEC + 3))
        count_up(ENC_VEC + 2, grad)
        grad_low = grad.astype(LOW)
        gl[rows, :] = grad_low
        normal, scale = norm_stats(x[rows, :])
        low = (normal * row(ENC_VEC) + row(ENC_VEC + 1)).astype(LOW)
        fl[rows, :] = low
        for half in range(2):
            cols = slice(half * width, (half + 1) * width)
            pre = dot_nn(low, whole(ENC_IN + half)) + enc_bias[half]
            share = gauss_share(pre)
            (kc, vc)[half][rows, :] = (pre * share).astype(LOW)
            back = dot_nt(grad_low, out_half(ENC_OUT, half)) * (share + pre * gauss_slope(pre))
            gbias[0:1, cols] += col_sum(back)
            back = back.astype(LOW)
            (dk, dv)[half][rows, :] = back
            grad = grad + dot_nt(back, whole(ENC_IN + half))
        count_up(ENC_VEC, grad * normal)
        count_up(ENC_VEC + 1, grad)
        grad = norm_back(grad, normal, scale, row(ENC_VEC))
        dm[rows, :] = grad
        dq[rows, :] = grad.astype(LOW)
        do[rows, :] = dot_nt(dq[rows, :], whole(ENC + 3)).astype(LOW)
        net.tick(AT_ENC_FEED_BACK, number)
    for half in range(2):
        weight_grad(ENC_IN + half, fl[...], (dk, dv)[half][...])
        put_out(ENC_OUT, half, dot_tn((kc, vc)[half][...], gl[...]))
    weight_grad(ENC + 3, o[...], dq[...])
    net.tick(AT_ENC_FFN_GRADS, 0)
    halves = [(start, size, patches) for start, size in wide_tiles]
    attend_back(
        q, k, v, lse, do, dq, dk, dv, dk_acc, dv_acc, halves, None, net.ticks(AT_ENC_BACK)
    )
    net.tick(AT_ENC_END, 0)
    weight_grad(ENC, xl[...], dq[...])
    weight_grad(ENC + 1, xl[...], dk[...])
    weight_grad(ENC + 2, xl[...], dv[...])
    net.tick(AT_ENC_GRADS, 0)
    for number, (start, size) in enumerate(wide_tiles):
        rows = pl.ds(start, size)
        grad = (
            dm[rows, :]
            + dot_nt(dq[rows, :], whole(ENC))
            + dot_nt(dk[rows, :], whole(ENC + 1))
            + dot_nt(dv[rows, :], whole(ENC + 2))
        )
        projected = dot_nt(feat[rows, :], project)
        count_up(AFFINE, grad * (projected - row(BN)) * bn_scale)
        count_up(AFFINE + 1, grad)
        low = (grad * (bn_scale * row(AFFINE))).astype(LOW)
        gl[rows, :] = low
        r2[rows, 0:channels] = dot_nn(low, project)
        net.tick(AT_PROJECT_BACK, number)
    out = pltpu.make_async_copy(r2.at[:, 0:channels], gfeat, done)
    out.start()
    columns = gvec[...].T
    lane = lax.broadcasted_iota(jnp.int32, columns.shape, 1)
    for index, first in ((0, ENC_HIDDEN), (1, DEC_HIDDEN)):
        for i, column in enumerate(bias_columns(gbias[index : index + 1, :])):
            columns = jnp.where(lane == first + i, column, columns)
    put(
        MISC,
        None,
        jnp.concatenate(
            [
                dot_tn(gl[...], feat[...]),
                columns,
                jnp.zeros((width, width - channels - VECTOR_ROWS), WIDE),
            ],
            axis=1,
        ),
    )
    net.flush()
    out.wait()


def math_buffers(patches, tags, width, hidden):
    wide = lambda *shape: pltpu.VMEM(shape, WIDE)
    low = lambda *shape: pltpu.VMEM(shape, LOW)
    rows, slots = (patches, width), (tags, width)
    return [
        wide(*rows), low(*rows), low(*rows), low(*rows), low(*rows), low(*rows), wide(patches, 128),
        wide(*rows), low(*rows),
        wide(*slots), low(*slots), low(*slots), low(*slots), low(*slots), low(*slots), wide(tags, 128),
        wide(*slots), low(*slots), low(*slots), low(*rows), low(*rows), low(*slots), wide(tags, 128),
        low(*rows), low(tags, hidden), low(*rows),
        low(*rows), low(*rows), low(*rows), low(*rows), wide(*rows),
        wide(128, patches), wide(128, patches), wide(VECTOR_ROWS, width), wide(VECTOR_ROWS, width),
        wide(8, hidden), pltpu.SemaphoreType.DMA(()),
    ]


class Quiet:
    def tick(self, name, number):
        pass

    def ticks(self, name):
        return ()

    def fence(self, name):
        pass

    def flush(self):
        pass


LAST = 9
HEAD = (
    ((E1, 0),),
    ((E1, 1), (D1, 0)),
    ((E1, 2), (E2, 0)),
    ((E1, 3), (D1, 1)),
)
PLAN = {
    (AT_ENCODE, 1): ((D1, 2),),
    (AT_ENC_ATTEND, 0): ((E2, 1), (D2, 0)),
    (AT_ENC_ATTEND, 1): ((D2, 1),),
    (AT_ENC_ATTEND, 2): ((E2, 2),),
    (AT_ENC_ATTEND, 3): ((D1, 3), (D2, 2)),
    (AT_SELF_ATTEND, 0): ((D3, 0),),
    (AT_SELF_ATTEND, 5): ((E2, 3),),
    (AT_SELF_ATTEND, 7): ((D3, 1),),
    (AT_ENC_FEED, 0): ((D2, 3),),
    (AT_ENC_FEED, 1): ((D3, 2),),
    (AT_CROSS_ATTEND, 3): ((D3, 3), (D2, LAST)),
    (AT_DEC_FEED, 1): ((D3, LAST),),
    (AT_DEC_FFN_GRADS, 0): ((RD3, 0),),
    (AT_CROSS_BACK, 1): ((RD3, 1),),
    (AT_CROSS_END, 0): ((RD3, 2), (D1, LAST)),
    (AT_CROSS_GRADS, 0): ((RD3, 3), (RD2, 0)),
    (AT_SELF_BACK, 4): ((RD2, 1),),
    (AT_SELF_END, 0): ((RD3, 4),),
    (AT_SELF_GRADS, 0): ((RD1, 0),),
    (AT_ENC_FEED_BACK, 0): ((RD2, 2),),
    (AT_ENC_FEED_BACK, 1): ((RD1, 1), (E1, LAST), (E2, LAST)),
    (AT_ENC_FFN_GRADS, 0): ((RD2, 3), (RE2, 0)),
    (AT_ENC_BACK, 2): ((RD1, 2),),
    (AT_ENC_BACK, 3): ((RD2, 4), (RE2, 1)),
    (AT_ENC_BACK, 4): ((RD1, 3),),
    (AT_ENC_BACK, 6): ((RE2, 2),),
    (AT_ENC_BACK, 7): ((RD1, 4),),
    (AT_ENC_END, 0): ((RE2, 3),),
    (AT_ENC_GRADS, 0): ((RA, 0),),
    (AT_PROJECT_BACK, 1): ((RE2, 4), (RA, 1)),
}
TAIL = (
    ((RB, 0),),
    ((RA, 2), (RB, 1)),
    ((RA, 3), (RB, 2)),
    ((RA, 4), (RB, 3)),
    ((RB, 4),),
)
GATHERS = {
    E1: ((MISC, 2, 0), (MISC + 2, 2, 1)),
    E2: ((ENC + 3, 3, 0), (ENC + 6, 2, 1)),
    D1: ((SELF, 2, 0), (SELF + 2, 2, 1)),
    D2: ((CROSS, 2, 0), (CROSS + 2, 2, 1)),
    D3: ((DEC_IN, 2, 0), (DEC_OUT, 2, 1)),
}
SCATTERS = {
    RD3: ((DEC_IN, DEC_IN, 2, 0, 0, 0), (DEC_OUT, DEC_OUT, 2, 1, 1, 0)),
    RD2: ((CROSS, CROSS, 2, 0, 2, 0), (CROSS + 2, CROSS + 2, 2, 1, 3, 0)),
    RD1: ((SELF, SELF, 2, 0, 4, 0), (SELF + 2, SELF + 2, 2, 1, 5, 0)),
    RE2: ((ENC + 3, ENC + 3, 3, 0, 0, 0), (ENC + 6, ENC + 6, 2, 1, 1, 0)),
    RA: ((SELF, ENC, 1, 0, 2, 0), (SELF + 1, ENC + 1, 1, 1, 3, 0), (SELF + 2, ENC + 2, 1, 2, 6, 0)),
    RB: ((MISC, MISC, 1, 1, 3, 1),),
}
INBOX = ((3, 0), (2, 1), (2, 0), (2, 1), (2, 0), (2, 1), (1, 2))


class Traffic:
    def __init__(self, place, w, inboxes, share, sems):
        gather_out, gather_in, scatter_out, scatter_in = sems
        self.groups, base = {}, 0
        for name, runs in GATHERS.items():
            self.groups[name] = Group([])
            for first, count, route in runs:
                pieces = (first, first + count)
                self.groups[name].runs.append(
                    Gather(w, place, pieces, ROUTES[route], gather_out, gather_in, base)
                )
                base += Gather.sems
        base = 0
        for name, runs in SCATTERS.items():
            self.groups[name] = Group([])
            for slot, piece, count, route, inbox, room in runs:
                self.groups[name].runs.append(
                    Scatter(
                        w, place, (slot, slot + count), ROUTES[route], inboxes[inbox], room, share, piece,
                        scatter_out, scatter_in, base,
                    )
                )
                base += Scatter.sems

    def run(self, steps):
        for name, step in steps:
            if step == LAST:
                self.groups[name].drain()
            else:
                self.groups[name].advance(step)

    def tick(self, name, number):
        self.run(PLAN.get((name, number), ()))

    def ticks(self, name):
        plans = [PLAN.get((name, number)) for number in range(HEADS)]
        return tuple(partial(self.run, plan) if plan else None for plan in plans)

    def fence(self, name):
        self.groups[name].finish()

    def flush(self):
        for plan in TAIL:
            self.run(plan)


POS_AT = 7


def fused_kernel(
    feat, ids, lens, cot, pos, proj, bn_given, bn_affine, enc_attn, enc_vec, enc_in, enc_hidden, enc_out,
    table, dec_self, dec_cross, dec_vec, dec_in, dec_hidden, dec_out, decoded, gfeat, share, *scratch
):
    w, cols, turned = scratch[:3]
    boxes = 3 + 4 * len(INBOX)
    inboxes = [scratch[3 + 4 * i : 7 + 4 * i] for i in range(len(INBOX))]
    sems, bufs = scratch[boxes : boxes + 5], scratch[boxes + 5 :]
    place = my_place()
    greet(place)
    width = w.shape[-1]
    rows = w.shape[-2]
    local = sems[0]
    channels = proj.shape[1]

    def own(first, count=1):
        return cube(w, (first, first + count), place, ())

    copies = [(enc_attn, own(ENC, 4)), (dec_self, own(SELF, 4)), (dec_cross, own(CROSS, 4))]
    for matrix, first in ((enc_in, ENC_IN), (dec_in, DEC_IN)):
        copies += [
            (matrix.at[:, half * width : (half + 1) * width], own(first + half).at[0])
            for half in range(2)
        ]
    for matrix, first in ((enc_out, ENC_OUT), (dec_out, DEC_OUT)):
        copies += [
            (matrix.at[half * rows : (half + 1) * rows, :], own(first + half).at[0])
            for half in range(2)
        ]
    copies = [
        pltpu.make_async_copy(source, target, local.at[number])
        for number, (source, target) in enumerate(copies)
    ]
    for copy in copies:
        copy.start()
    fetch = pltpu.make_async_copy(pos, bufs[-POS_AT], local.at[11])
    fetch.start()
    cols[...] = jnp.zeros_like(cols)
    for part, first in ((bn_given, BN), (bn_affine, AFFINE), (enc_vec, ENC_VEC), (dec_vec, DEC_VEC)):
        cols[first : first + part.shape[0], 0:rows] = part[...].astype(WIDE)
    for part, first in ((enc_hidden, ENC_HIDDEN), (dec_hidden, DEC_HIDDEN)):
        for half in range(2):
            cols[first + half : first + half + 1, 0:rows] = part[0:1, half * rows : (half + 1) * rows].astype(WIDE)
    turned[...] = cols[...].T[0:rows, :]
    turned[:, TABLE : TABLE + VOCAB] = table[...].astype(WIDE)
    first = jnp.concatenate(
        [proj[...], turned[...].astype(LOW), jnp.zeros((rows, width - channels - VECTOR_ROWS), LOW)], axis=1
    )
    own(MISC)[...] = first[None]
    await_greetings()
    for copy in copies:
        copy.wait()
    net = Traffic(place, w, inboxes, share, sems[1:])
    for plan in HEAD:
        net.run(plan)

    def put(piece, half, value):
        slot = piece - ENC + SELF if ENC <= piece < ENC + 3 else piece
        if half is None:
            w[slot] = value.reshape(BITS + (rows, width)).astype(LOW)
        else:
            w[slot, half] = value.reshape(BITS[1:] + (rows, width)).astype(LOW)

    fetch.wait()
    layer_math(feat, ids, lens[0], cot, w, decoded, gfeat, put, net, bufs)


def plain_kernel(feat, ids, lens, cot, pos, w, decoded, gfeat, g, *bufs):
    width = w.shape[-1]

    def put(piece, half, value):
        if half is None:
            g[piece] = value.reshape(g.shape[1:]).astype(LOW)
        else:
            g[piece, half] = value.reshape(g.shape[2:]).astype(LOW)

    pltpu.sync_copy(pos, bufs[-POS_AT])
    layer_math(feat, ids, lens[0], cot, w, decoded, gfeat, put, Quiet(), bufs)


VMEM = pl.BlockSpec(memory_space=pltpu.VMEM)
SMEM = pl.BlockSpec(memory_space=pltpu.SMEM)
ANY = pl.BlockSpec(memory_space=pl.ANY)
LIMIT = 63 << 20


def split_update(features, tag_ids, tag_lengths, out_cot, parameters):
    (
        proj, bn_given, bn_affine, enc_attn, enc_vec, enc_in, enc_hidden, enc_out,
        table, dec_self, dec_cross, dec_vec, dec_in, dec_hidden, dec_out,
    ) = parameters
    patches, channels = features.shape[1:]
    tags, width = out_cot.shape[1:]
    rows = width // BLOCKS
    pos = jnp.asarray(position_table(max(patches, tags), width))
    sems = (
        Gather.sems * sum(len(runs) for runs in GATHERS.values()),
        Scatter.sems * sum(len(runs) for runs in SCATTERS.values()),
    )
    boxes = [
        pltpu.VMEM(shape, LOW)
        for count, route in INBOX
        for shape in inbox_shapes(count, ROUTES[route], rows, width)
    ]
    dma = pltpu.SemaphoreType.DMA
    decoded, gfeat, share = pl.pallas_call(
        fused_kernel,
        in_specs=[VMEM, VMEM, SMEM, VMEM, ANY, VMEM, VMEM, VMEM, ANY, VMEM, ANY, VMEM, ANY]
        + [VMEM, ANY, ANY, VMEM, ANY, VMEM, ANY],
        out_shape=(
            jax.ShapeDtypeStruct((tags, width), LOW),
            jax.ShapeDtypeStruct((patches, channels), WIDE),
            jax.ShapeDtypeStruct((PIECES, rows, width), WIDE),
        ),
        out_specs=(VMEM, ANY, VMEM),
        scratch_shapes=[
            pltpu.VMEM((PIECES,) + BITS + (rows, width), LOW),
            pltpu.VMEM((VECTOR_ROWS, 128), WIDE),
            pltpu.VMEM((rows, VECTOR_ROWS), WIDE),
            *boxes,
            dma((12,)),
            dma((sems[0],)),
            dma((sems[0],)),
            dma((sems[1],)),
            dma((sems[1],)),
            *math_buffers(patches, tags, width, enc_in.shape[1]),
        ],
        compiler_params=pltpu.CompilerParams(
            collective_id=0, has_side_effects=True, vmem_limit_bytes=LIMIT
        ),
        name="layers",
    )(
        features[0], tag_ids, tag_lengths, out_cot[0], pos, proj.T, bn_given, bn_affine, enc_attn, enc_vec,
        enc_in, enc_hidden.reshape(1, -1), enc_out, table.T, dec_self, dec_cross, dec_vec, dec_in,
        dec_hidden.reshape(1, -1), dec_out,
    )
    outs = finish(decoded, gfeat, share, channels)
    return (
        outs[0][None],
        outs[1][None],
        outs[2].T,
        *outs[3:7],
        outs[7].reshape(-1),
        outs[8],
        outs[9].T,
        *outs[10:14],
        outs[14].reshape(-1),
        outs[15],
    )


def finish_kernel(
    decoded, gfeat, share, decoded_out, gfeat_out, proj, affine, enc_attn, enc_vec, enc_in, enc_hidden,
    enc_out, table, dec_self, dec_cross, dec_vec, dec_in, dec_hidden, dec_out
):
    rows, width = share.shape[1:]
    channels = proj.shape[1]
    decoded_out[...] = decoded[...]
    gfeat_out[...] = gfeat[...]
    enc_attn[...] = share[ENC : ENC + 4]
    dec_self[...] = share[SELF : SELF + 4]
    dec_cross[...] = share[CROSS : CROSS + 4]
    for half in range(2):
        enc_in[:, half * width : (half + 1) * width] = share[ENC_IN + half]
        dec_in[:, half * width : (half + 1) * width] = share[DEC_IN + half]
        enc_out[half * rows : (half + 1) * rows, :] = share[ENC_OUT + half]
        dec_out[half * rows : (half + 1) * rows, :] = share[DEC_OUT + half]
    columns = share[MISC]
    proj[...] = columns[:, 0:channels]
    table[...] = columns[:, channels + TABLE : channels + TABLE + VOCAB]
    vectors = jnp.concatenate(
        [columns[:, channels : channels + VECTOR_ROWS], jnp.zeros((128 - rows, VECTOR_ROWS), WIDE)],
        axis=0,
    ).T[:, 0:rows]
    for part, first in ((affine, AFFINE), (enc_vec, ENC_VEC), (dec_vec, DEC_VEC)):
        part[...] = vectors[first : first + part.shape[0]]
    for part, first in ((enc_hidden, ENC_HIDDEN), (dec_hidden, DEC_HIDDEN)):
        part[...] = jnp.concatenate([vectors[first : first + 1], vectors[first + 1 : first + 2]], axis=1)


def finish(decoded, gfeat, share, channels):
    rows, width = share.shape[1:]
    shape = lambda *dims: jax.ShapeDtypeStruct(dims, WIDE)
    return pl.pallas_call(
        finish_kernel,
        in_specs=[VMEM] * 3,
        out_shape=(
            jax.ShapeDtypeStruct(decoded.shape, decoded.dtype),
            jax.ShapeDtypeStruct(gfeat.shape, gfeat.dtype),
            shape(rows, channels),
            shape(2, rows),
            shape(4, rows, width),
            shape(5, rows),
            shape(rows, 2 * width),
            shape(1, 2 * rows),
            shape(2 * rows, width),
            shape(rows, VOCAB),
            shape(4, rows, width),
            shape(4, rows, width),
            shape(7, rows),
            shape(rows, 2 * width),
            shape(1, 2 * rows),
            shape(2 * rows, width),
        ),
        out_specs=(VMEM,) * 16,
        name="finish",
    )(decoded, gfeat, share)


def gathered_update(features, tag_ids, tag_lengths, out_cot, parameters):
    dims = (1, 1, 1, 1, 1, 0, 0, 0, 1, 1, 1, 1, 0, 0, 0)
    full = [lax.all_gather(a, AXES, axis=d, tiled=True) for a, d in zip(parameters, dims)]
    (
        proj, bn_given, bn_affine, enc_attn, enc_vec, enc_in, enc_hidden, enc_out,
        table, dec_self, dec_cross, dec_vec, dec_in, dec_hidden, dec_out,
    ) = full
    patches, channels = features.shape[1:]
    tags, width = out_cot.shape[1:]
    rows = width // BLOCKS

    def swap(matrix):
        return matrix.reshape((BLOCKS, 2, -1) + matrix.shape[1:]).swapaxes(0, 1).reshape((2, -1) + matrix.shape[1:])

    def halves(matrix):
        return jnp.stack([matrix[:, :width], matrix[:, width:]])

    columns = jnp.concatenate(
        [proj, bn_given, bn_affine, enc_vec, dec_vec, table, swap(enc_hidden), swap(dec_hidden)], axis=0
    )
    columns = jnp.pad(columns, ((0, width - columns.shape[0]), (0, 0))).T
    stack = jnp.concatenate(
        [columns[None], enc_attn, halves(enc_in), swap(enc_out), dec_self, dec_cross]
        + [halves(dec_in), swap(dec_out)],
        axis=0,
    ).reshape((PIECES,) + BITS + (rows, width))
    decoded, gfeat, grads = pl.pallas_call(
        plain_kernel,
        in_specs=[VMEM, VMEM, SMEM, VMEM, ANY, VMEM],
        out_shape=(
            jax.ShapeDtypeStruct((tags, width), LOW),
            jax.ShapeDtypeStruct((patches, channels), WIDE),
            jax.ShapeDtypeStruct(stack.shape, LOW),
        ),
        out_specs=(VMEM, ANY, VMEM),
        scratch_shapes=math_buffers(patches, tags, width, enc_in.shape[1]),
        compiler_params=pltpu.CompilerParams(vmem_limit_bytes=LIMIT),
        name="layers",
    )(features[0], tag_ids, tag_lengths, out_cot[0], jnp.asarray(position_table(max(patches, tags), width)), stack)
    grads = grads.reshape(PIECES, width, width).astype(WIDE)
    columns = grads[MISC].T
    vectors = columns[channels:]

    def join(pair):
        return pair.reshape((2, BLOCKS, -1) + pair.shape[2:]).swapaxes(0, 1).reshape((-1,) + pair.shape[2:])

    def wide(pair):
        return jnp.concatenate([pair[0], pair[1]], axis=1)

    totals = (
        (columns[:channels], 1),
        (vectors[AFFINE : AFFINE + 2], 1),
        (grads[ENC : ENC + 4], 1),
        (vectors[ENC_VEC:DEC_VEC], 1),
        (wide(grads[ENC_IN:ENC_OUT]), 0),
        (join(vectors[ENC_HIDDEN : ENC_HIDDEN + 2]), 0),
        (join(grads[ENC_OUT:SELF]), 0),
        (vectors[TABLE : TABLE + VOCAB], 1),
        (grads[SELF:CROSS], 1),
        (grads[CROSS:DEC_IN], 1),
        (vectors[DEC_VEC:TABLE], 1),
        (wide(grads[DEC_IN:DEC_OUT]), 0),
        (join(vectors[DEC_HIDDEN : DEC_HIDDEN + 2]), 0),
        (join(grads[DEC_OUT:PIECES]), 0),
    )
    return (
        decoded[None],
        gfeat[None],
        *[lax.psum_scatter(a, AXES, scatter_dimension=d, tiled=True) for a, d in totals],
    )


def body(mesh_shape, features, tag_ids, tag_lengths, out_cot, *parameters):
    update = split_update if mesh_shape == (16, 2) else gathered_update
    return update(features, tag_ids, tag_lengths, out_cot, parameters)


def solution(mesh):
    placed = (
        P(("wide", "narrow"), None, None),
        P(("wide", "narrow"), None),
        P(("wide", "narrow")),
        P(("wide", "narrow"), None, None),
        P(None, ("wide", "narrow")),
        P(None, ("wide", "narrow")),
        P(None, ("wide", "narrow")),
        P(None, ("wide", "narrow"), None),
        P(None, ("wide", "narrow")),
        P(("wide", "narrow"), None),
        P(("wide", "narrow")),
        P(("wide", "narrow"), None),
        P(None, ("wide", "narrow")),
        P(None, ("wide", "narrow"), None),
        P(None, ("wide", "narrow"), None),
        P(None, ("wide", "narrow")),
        P(("wide", "narrow"), None),
        P(("wide", "narrow")),
        P(("wide", "narrow"), None),
    )
    return jax.shard_map(
        partial(body, tuple(mesh.shape[axis] for axis in AXES)),
        mesh=mesh,
        in_specs=placed,
        out_specs=(
            P(("wide", "narrow"), None, None),
            P(("wide", "narrow"), None, None),
            P(None, ("wide", "narrow")),
            P(None, ("wide", "narrow")),
            P(None, ("wide", "narrow"), None),
            P(None, ("wide", "narrow")),
            P(("wide", "narrow"), None),
            P(("wide", "narrow")),
            P(("wide", "narrow"), None),
            P(None, ("wide", "narrow")),
            P(None, ("wide", "narrow"), None),
            P(None, ("wide", "narrow"), None),
            P(None, ("wide", "narrow")),
            P(("wide", "narrow"), None),
            P(("wide", "narrow")),
            P(("wide", "narrow"), None),
        ),
        check_vma=False,
    )
```
